32 devices in a mesh: dp: 4 (over z), fsdp: 8 (over y, x, core).
Axes of the slice: x: 2, y: 2, z: 4, core: 2. Of those that a mesh axis runs over, the one named last changes fastest.
Arguments:
- inputs: bfloat16 [128, 256, 512], P(('dp', 'fsdp')), may hold values from -6 to 6
- memory: bfloat16 [128, 512, 512], P(('dp', 'fsdp'))
- cotangent: bfloat16 [128, 256, 512], P(('dp', 'fsdp')), may hold values from -6 to 6
- lengths: int32 [128], P(('dp', 'fsdp')), may hold values from 32 to 256
- mem_lengths: int32 [128], P(('dp', 'fsdp')), may hold values from 64 to 512
- attn_weights: float32 [8, 512, 512], P(None, ('dp', 'fsdp'))
- ffn_in: float32 [512, 2048], P(('dp', 'fsdp')), may hold values from -0.25 to 0.25
- ffn_out: float32 [2048, 512], P(('dp', 'fsdp')), may hold values from -0.125 to 0.125
- vectors: float32 [17, 512], P(None, ('dp', 'fsdp'))
- attn_first: float32 [8, 512, 512], P(None, ('dp', 'fsdp')), may hold values from -0.0029296875 to 0.0029296875
- attn_second: float32 [8, 512, 512], P(None, ('dp', 'fsdp')), may hold values from 2.3792484e-07 to 9.5169935e-07
- ffn_in_first: float32 [512, 2048], P(('dp', 'fsdp')), may hold values from -0.0029296875 to 0.0029296875
- ffn_in_second: float32 [512, 2048], P(('dp', 'fsdp')), may hold values from 2.855098e-08 to 1.1896242e-07
- ffn_out_first: float32 [2048, 512], P(('dp', 'fsdp')), may hold values from -0.0029296875 to 0.0029296875
- ffn_out_second: float32 [2048, 512], P(('dp', 'fsdp')), may hold values from 2.3792484e-07 to 9.5169935e-07
- vector_first: float32 [17, 512], P(None, ('dp', 'fsdp')), may hold values from -0.0029296875 to 0.0029296875
- vector_second: float32 [17, 512], P(None, ('dp', 'fsdp')), may hold values from 2.3792484e-07 to 9.5169935e-07
Outputs:
- output: float32 [128, 256, 512], P(('dp', 'fsdp'))
- input_grad: float32 [128, 256, 512], P(('dp', 'fsdp'))
- memory_grad: float32 [128, 512, 512], P(('dp', 'fsdp'))
- grad_norm: float32 [1], replicated
- new_attn_weights: float32 [8, 512, 512], P(None, ('dp', 'fsdp'))
- new_attn_first: float32 [8, 512, 512], P(None, ('dp', 'fsdp'))
- new_attn_second: float32 [8, 512, 512], P(None, ('dp', 'fsdp'))
- new_ffn_in: float32 [512, 2048], P(('dp', 'fsdp'))
- new_ffn_in_first: float32 [512, 2048], P(('dp', 'fsdp'))
- new_ffn_in_second: float32 [512, 2048], P(('dp', 'fsdp'))
- new_ffn_out: float32 [2048, 512], P(('dp', 'fsdp'))
- new_ffn_out_first: float32 [2048, 512], P(('dp', 'fsdp'))
- new_ffn_out_second: float32 [2048, 512], P(('dp', 'fsdp'))
- new_vectors: float32 [17, 512], P(None, ('dp', 'fsdp'))
- new_vector_first: float32 [17, 512], P(None, ('dp', 'fsdp'))
- new_vector_second: float32 [17, 512], P(None, ('dp', 'fsdp'))
The draws below stay inside these ranges and needn't reach their ends.
Inputs may be any that keep to these rules, and one draw needn't show every extreme that they name: `lengths`: positions at or past a sequence's length are padding. `mem_lengths`: memory positions at or past this length are padding.
All inputs are finite; a program needn't handle non-finite values.
Results may differ from the reference program's by a relative error of at most 0.018.
The reference program's roundings to bfloat16 on the way count: a program that leaves them out, or rounds other values in their place, can miss the bound.
Values may be sent and summed in bfloat16 or wider, within the bound.
No kernel may reach another device: no remote copies, remote signals or barrier semaphores. Data moves between devices by JAX's collectives and lax.ppermute only.
A program may use at most 192 MiB of HBM per device.

```python
import math
import jax
import jax.numpy as jnp
from jax import lax

D = 512
HEADS = 8
HEAD_DIM = 64
FF = 2048
LEN = 256
MEM = 512
STEP = 5
VECS = 17
SEQS = 128
PARAMS = 4203008


def draw_attn_weights(key, part):
    base = jnp.clip(jax.random.normal(key, (8, D, D), jnp.float32), -6.0, 6.0) * D ** (-0.5)
    factor = jnp.array([1.5, 1.0, 1.0, 3.0, 1.5, 1.0, 1.0, 3.0], jnp.float32)
    return base * factor[:, None, None]


def draw_vectors(key, part):
    noise = jnp.clip(jax.random.normal(jax.random.fold_in(key, 11), (VECS, D), jnp.float32), -5.0, 5.0)
    ramp = jnp.arange(D).astype(jnp.float32) / (D - 1)
    gain_factor = 0.3 + 2.4 * ramp
    gains = gain_factor[None, :] * (1.0 + 0.1 * noise[0:6:2]) - 1.0
    table = 0.3 * noise
    return table.at[0:6:2].set(gains)


def draw_memory(key, part):
    noise = jnp.clip(jax.random.normal(jax.random.fold_in(key, 23), (SEQS, MEM, D), jnp.float32), -6.0, 6.0)
    ramp = jnp.arange(D).astype(jnp.float32) / (D - 1)
    scale = 0.5 + ramp
    return (noise * scale[None, None, :]).astype(jnp.bfloat16)


def set_ends(values, key, low, high):
    spot = [jax.random.randint(jax.random.fold_in(key, axis), (), 0, length) for axis, length in enumerate(values.shape)]
    main_axis = values.shape.index(max(values.shape))
    beside = spot[:main_axis] + [(spot[main_axis] + 1) % values.shape[main_axis]] + spot[main_axis + 1:]
    return values.at[tuple(spot)].set(low).at[tuple(beside)].set(high)


def block_scale(rng, dims, cuts, smallest, top_value):
    loudness, own = 1.0, jax.random.fold_in(rng, 6)
    for position, shards_of in cuts:
        heights = jnp.exp(jax.random.uniform(jax.random.fold_in(own, position), (shards_of,), jnp.float32, smallest / len(cuts), top_value / len(cuts)))
        loudness = loudness * jnp.repeat(heights, dims[position] // shards_of).reshape([-1 if axis == position else 1 for axis in range(len(dims))])
    return loudness


def bell_draw(key, shape, scale, bound, shards=(), held_as=jnp.bfloat16):
    level = block_scale(key, shape, shards, -0.22, 0.18) if shards else 1.0
    drawn = jax.random.normal(key, shape, jnp.float32) * scale * level
    return jnp.minimum(jnp.maximum(drawn, -bound), bound).astype(held_as)


def setup_inputs(seed: int = 0) -> dict:
    key_of = jax.random.split(jax.random.key(seed), 18)
    inputs = bell_draw(key_of[0], (SEQS, LEN, D), 1.0, 6.0, ((0, 32),))
    memory = draw_memory(jax.random.fold_in(key_of[17], 71), 0)
    cotangent = bell_draw(key_of[2], (SEQS, LEN, D), 1.0, 6.0, ((0, 32),))
    lengths = set_ends(jax.random.randint(key_of[3], (SEQS,), LEN // 8, LEN + 1), jax.random.fold_in(key_of[3], 1), LEN // 8, LEN).astype(jnp.int32)
    mem_lengths = set_ends(jax.random.randint(key_of[4], (SEQS,), MEM // 8, MEM + 1), jax.random.fold_in(key_of[4], 1), MEM // 8, MEM).astype(jnp.int32)
    attn_weights = draw_attn_weights(jax.random.fold_in(key_of[17], 71), 0)
    ffn_in = bell_draw(key_of[6], (D, FF), D ** -0.5, 0.25, ((0, 32),), jnp.float32)
    ffn_out = bell_draw(key_of[7], (FF, D), FF ** -0.5, 0.125, ((0, 32),), jnp.float32)
    vectors = draw_vectors(jax.random.fold_in(key_of[17], 71), 0)
    attn_first = bell_draw(key_of[9], (8, D, D), PARAMS ** -0.5, 0.0029296875, ((1, 32),), jnp.float32)
    attn_second = jnp.clip(jnp.exp(math.log(9.516993486613501e-07) - 1.3862944 * jax.random.uniform(key_of[10], (8, D, D), jnp.float32) ** block_scale(key_of[10], (8, D, D), ((1, 32),), -0.2, 0.2)), 2.3792483716533752e-07, 9.516993486613501e-07)
    ffn_in_first = bell_draw(key_of[11], (D, FF), PARAMS ** -0.5, 0.0029296875, ((0, 32),), jnp.float32)
    ffn_in_second = jnp.clip(jnp.exp(math.log(1.1896241858266876e-07) - 1.4271164 * jax.random.uniform(key_of[12], (D, FF), jnp.float32) ** block_scale(key_of[12], (D, FF), ((0, 32),), -0.2, 0.2)), 2.8550980246677682e-08, 1.1896241858266876e-07)
    ffn_out_first = bell_draw(key_of[13], (FF, D), PARAMS ** -0.5, 0.0029296875, ((0, 32),), jnp.float32)
    ffn_out_second = jnp.clip(jnp.exp(math.log(9.516993486613501e-07) - 1.3862944 * jax.random.uniform(key_of[14], (FF, D), jnp.float32) ** block_scale(key_of[14], (FF, D), ((0, 32),), -0.2, 0.2)), 2.3792483716533752e-07, 9.516993486613501e-07)
    vector_first = bell_draw(key_of[15], (VECS, D), PARAMS ** -0.5, 0.0029296875, ((1, 32),), jnp.float32)
    vector_second = jnp.clip(jnp.exp(math.log(9.516993486613501e-07) - 1.3862944 * jax.random.uniform(key_of[16], (VECS, D), jnp.float32) ** block_scale(key_of[16], (VECS, D), ((1, 32),), -0.2, 0.2)), 2.3792483716533752e-07, 9.516993486613501e-07)
    return {"inputs": inputs, "memory": memory, "cotangent": cotangent, "lengths": lengths, "mem_lengths": mem_lengths, "attn_weights": attn_weights, "ffn_in": ffn_in, "ffn_out": ffn_out, "vectors": vectors, "attn_first": attn_first, "attn_second": attn_second, "ffn_in_first": ffn_in_first, "ffn_in_second": ffn_in_second, "ffn_out_first": ffn_out_first, "ffn_out_second": ffn_out_second, "vector_first": vector_first, "vector_second": vector_second}


@jax.custom_vjp
def low(v):
    return lax.optimization_barrier(v.astype(jnp.bfloat16)).astype(jnp.float32)

@jax.custom_vjp
def low_back(v):
    return v

def low_keep(v):
    return (low(v), None)

def low_pass(kept, grad):
    return (grad,)

def back_keep(v):
    return (v, None)

def back_low(kept, grad):
    return (low(grad),)
low.defvjp(low_keep, low_pass)
low_back.defvjp(back_keep, back_low)

def layer_norm(values, gain, shift):
    center = values - lax.optimization_barrier(jnp.mean(values, -1, keepdims=True))
    spread = lax.optimization_barrier(jnp.mean(center * center, -1, keepdims=True))
    return center * lax.rsqrt(spread + 1e-05) * (1.0 + gain) + shift

def matmul_high(left, right):
    return jnp.matmul(left, right, precision=lax.Precision.HIGHEST)

def attend(queries, keys, values, mask):
    scores = jnp.einsum('bqhe,bkhe->bhqk', queries, keys, precision=lax.Precision.HIGHEST) * HEAD_DIM ** (-0.5)
    scores = low_back(scores)
    scores = jnp.where(mask, scores, -1e+30)
    probs = jax.nn.softmax(scores, -1)
    return jnp.einsum('bhqk,bkhe->bqhe', low(probs), values, precision=lax.Precision.HIGHEST)

def split_heads(flat):
    return flat.reshape(flat.shape[0], flat.shape[1], HEADS, HEAD_DIM)

def join_heads(grid):
    return grid.reshape(grid.shape[0], grid.shape[1], HEADS * HEAD_DIM)

def forward(attn_weights, ffn_in, ffn_out, vectors, inputs, memory, lengths, mem_lengths):
    weights = low(attn_weights)
    first_proj = low(ffn_in)
    second_proj = low(ffn_out)
    table = low(vectors)
    length = inputs.shape[1]
    mem_len = memory.shape[1]
    positions = jnp.arange(length)
    valid = positions[None, :] < lengths[:, None]
    self_mask = (positions[:, None] >= positions[None, :])[None, None] & valid[:, None, None, :]
    cross_mask = (jnp.arange(mem_len)[None, :] < mem_lengths[:, None])[:, None, None, :]
    act_one = low(layer_norm(inputs, table[0], table[1]))
    query_self = low_back(low(matmul_high(act_one, weights[0]) + table[6]))
    key_self = low_back(low(matmul_high(act_one, weights[1])))
    value_self = low_back(low(matmul_high(act_one, weights[2]) + table[7]))
    mixed_self = attend(split_heads(query_self), split_heads(key_self), split_heads(value_self), self_mask)
    mixed_self = low_back(low(join_heads(mixed_self)))
    resid_one = inputs + low_back(matmul_high(mixed_self, weights[3]) + table[8])
    act_two = low(layer_norm(resid_one, table[2], table[3]))
    query_cross = low_back(low(matmul_high(act_two, weights[4]) + table[9]))
    key_cross = low_back(low(matmul_high(memory, weights[5])))
    value_cross = low_back(low(matmul_high(memory, weights[6]) + table[10]))
    mixed_cross = attend(split_heads(query_cross), split_heads(key_cross), split_heads(value_cross), cross_mask)
    mixed_cross = low_back(low(join_heads(mixed_cross)))
    resid_two = resid_one + low_back(matmul_high(mixed_cross, weights[7]) + table[11])
    act_three = low(layer_norm(resid_two, table[4], table[5]))
    hidden_pre = low_back(matmul_high(act_three, first_proj) + table[13:].reshape(FF))
    hidden = low(jax.nn.gelu(hidden_pre, approximate=False))
    return resid_two + low_back(matmul_high(hidden, second_proj) + table[12])

def adam_update(weight, grad, first, second, clip_scale, step, rate):
    clipped = grad * clip_scale
    first_new = 0.5 * first + 0.5 * clipped
    second_new = 0.55 * second + 0.45 * clipped * clipped
    fix_first = 1.0 - jnp.power(0.5, step)
    fix_second = 1.0 - jnp.power(0.55, step)
    weight_new = weight - rate * (first_new / fix_first / (jnp.sqrt(second_new / fix_second) + 1e-08) + 0.01 * weight)
    return (weight_new, first_new, second_new)

def reference(inputs, memory, cotangent, lengths, mem_lengths, attn_weights, ffn_in, ffn_out, vectors, attn_first, attn_second, ffn_in_first, ffn_in_second, ffn_out_first, ffn_out_second, vector_first, vector_second):
    group = math.gcd(SEQS, max(1, 4096 // LEN))
    count = SEQS // group

    def regroup(array):
        return array.reshape((count, group) + array.shape[1:])

    def one_group(totals, pieces):
        piece_in, piece_mem, piece_cot, piece_len, piece_mlen = pieces

        def closed(weights, first_proj, second_proj, table, values, mem_values):
            return forward(weights, first_proj, second_proj, table, values, mem_values, piece_len, piece_mlen)
        result, pullback = jax.vjp(closed, attn_weights, ffn_in, ffn_out, vectors, piece_in.astype(jnp.float32), piece_mem.astype(jnp.float32))
        valid = (jnp.arange(LEN)[None, :] < piece_len[:, None]).astype(jnp.float32)
        grads = pullback(piece_cot.astype(jnp.float32) * valid[:, :, None])
        new_totals = (totals[0] + grads[0], totals[1] + grads[1], totals[2] + grads[2], totals[3] + grads[3])
        return (new_totals, (result, grads[4], grads[5]))
    zeros = (jnp.zeros_like(attn_weights), jnp.zeros_like(ffn_in), jnp.zeros_like(ffn_out), jnp.zeros_like(vectors))
    totals, stacked = lax.scan(one_group, zeros, (regroup(inputs), regroup(memory), regroup(cotangent), regroup(lengths), regroup(mem_lengths)))
    output = stacked[0].reshape(SEQS, LEN, D)
    input_grad = stacked[1].reshape(SEQS, LEN, D)
    memory_grad = stacked[2].reshape(SEQS, MEM, D)
    squares = jnp.sum(totals[0] * totals[0]) + jnp.sum(totals[1] * totals[1]) + jnp.sum(totals[2] * totals[2]) + jnp.sum(totals[3] * totals[3])
    grad_norm = jnp.sqrt(squares)
    clip_scale = jnp.minimum(1.0, 1.0 / (grad_norm + 1e-06))
    step = jnp.float32(STEP)
    attn_new = adam_update(attn_weights, totals[0], attn_first, attn_second, clip_scale, step, 0.04)
    first_new = adam_update(ffn_in, totals[1], ffn_in_first, ffn_in_second, clip_scale, step, 0.04)
    second_new = adam_update(ffn_out, totals[2], ffn_out_first, ffn_out_second, clip_scale, step, 0.04)
    table_new = adam_update(vectors, totals[3], vector_first, vector_second, clip_scale, step, 0.25)
    return (output, input_grad, memory_grad, grad_norm.reshape(1), attn_new[0], attn_new[1], attn_new[2], first_new[0], first_new[1], first_new[2], second_new[0], second_new[1], second_new[2], table_new[0], table_new[1], table_new[2])
```

```python
from functools import partial

import jax
import jax.numpy as jnp
from jax import lax
from jax.sharding import PartitionSpec as P

HEADS = 8
HEAD_DIM = 64
STEP = 5


def layer_norm(values, gain, shift):
    center = values - jnp.mean(values, -1, keepdims=True)
    spread = jnp.mean(center * center, -1, keepdims=True)
    return center * lax.rsqrt(spread + 1e-05) * (1.0 + gain) + shift


def plain_dot(left, right):
    return jnp.dot(left, right, preferred_element_type=jnp.float32)


def left_dot(left, right):
    return lax.dot_general(
        left, right, (((0,), (0,)), ((), ())), preferred_element_type=jnp.float32
    )


def right_dot(left, right):
    return lax.dot_general(
        left, right, (((1,), (1,)), ((), ())), preferred_element_type=jnp.float32
    )


def column_sum(values):
    return jnp.sum(values.astype(jnp.float32), 0)


def score_block(queries, keys, mask):
    scores = jnp.einsum(
        "sqhe,skhe->shqk", queries, keys, preferred_element_type=jnp.float32
    ) * HEAD_DIM ** (-0.5)
    return jnp.where(mask, scores, -1e30)


def attend_forward(queries, keys, values, mask):
    scores = score_block(queries, keys, mask)
    top = jnp.max(scores, -1, keepdims=True)
    expo = jnp.exp(scores - top)
    total = jnp.sum(expo, -1, keepdims=True)
    probs = (expo / total).astype(jnp.bfloat16)
    mixed = jnp.einsum("shqk,skhe->sqhe", probs, values, preferred_element_type=jnp.float32)
    return (mixed, top + jnp.log(total))


def attend_backward(queries, keys, values, mask, logsum, grad_mixed):
    scores = score_block(queries, keys, mask)
    probs = jnp.exp(scores - logsum)
    grad_probs = jnp.einsum(
        "sqhe,skhe->shqk", grad_mixed, values, preferred_element_type=jnp.float32
    )
    inner = jnp.sum(probs * grad_probs, -1, keepdims=True)
    grad_scores = (probs * (grad_probs - inner)).astype(jnp.bfloat16)
    scale = HEAD_DIM ** (-0.5)
    grad_query = (
        jnp.einsum("shqk,skhe->sqhe", grad_scores, keys, preferred_element_type=jnp.float32) * scale
    )
    grad_key = (
        jnp.einsum("shqk,sqhe->skhe", grad_scores, queries, preferred_element_type=jnp.float32)
        * scale
    )
    grad_value = jnp.einsum(
        "shqk,sqhe->skhe",
        probs.astype(jnp.bfloat16),
        grad_mixed,
        preferred_element_type=jnp.float32,
    )
    return (grad_query, grad_key, grad_value)


def adam_update(weight, grad, first, second, clip_scale, step, rate):
    clipped = grad * clip_scale
    first_new = 0.5 * first + 0.5 * clipped
    second_new = 0.55 * second + 0.45 * clipped * clipped
    fix_first = 1.0 - jnp.power(0.5, step)
    fix_second = 1.0 - jnp.power(0.55, step)
    weight_new = weight - rate * (
        first_new / fix_first / (jnp.sqrt(second_new / fix_second) + 1e-08) + 0.01 * weight
    )
    return (weight_new, first_new, second_new)


AXES = ("dp", "fsdp")


class Grid:
    def __init__(self, dp, fsdp):
        self.sizes = (dp, fsdp // 2, 2)
        self.strides = (fsdp, 2, 1)
        self.devices = dp * fsdp
        index = lax.axis_index("fsdp")
        self.place = (lax.axis_index("dp"), index // 2, index % 2)

    def swap(self, values, stage, step):
        stride = self.strides[stage]
        pairs = [(i, i ^ (step * stride)) for i in range(self.devices)]
        return lax.ppermute(values, AXES, pairs)

    def gather(self, chunk):
        held = chunk
        for stage in range(3):
            size, place = self.sizes[stage], self.place[stage]
            parts = [held] + [self.swap(held, stage, step) for step in range(1, size)]
            if size == 2:
                first = jnp.where(place == 0, parts[0], parts[1])
                second = jnp.where(place == 0, parts[1], parts[0])
                held = jnp.stack([first, second], stage)
            else:
                whole = jnp.zeros(held.shape[:stage] + (size,) + held.shape[stage:], held.dtype)
                for step in range(size):
                    whole = lax.dynamic_update_index_in_dim(whole, parts[step], place ^ step, stage)
                held = whole
        return held

    def scatter(self, parts):
        held = parts
        for stage in (2, 1, 0):
            size, place = self.sizes[stage], self.place[stage]
            total = lax.dynamic_index_in_dim(held, place, stage, False).astype(jnp.float32)
            for step in range(1, size):
                piece = lax.dynamic_index_in_dim(held, place ^ step, stage, False)
                total = total + self.swap(piece.astype(jnp.bfloat16), stage, step).astype(jnp.float32)
            held = total
        return held


def local(
    grid,
    inputs,
    memory,
    cotangent,
    lengths,
    mem_lengths,
    attn_weights,
    ffn_in,
    ffn_out,
    vectors,
    attn_first,
    attn_second,
    ffn_in_first,
    ffn_in_second,
    ffn_out_first,
    ffn_out_second,
    vector_first,
    vector_second,
):
    width = inputs.shape[2]
    own = attn_weights.shape[1]
    spots = grid.sizes

    def fold(array):
        return array.reshape(-1, width)

    vec_count = vectors.shape[0]
    table_rows = -(-vec_count * own // width)

    def fold_table(array, lead=()):
        flat = array.reshape(lead + (vec_count * own,))
        pad = [(0, 0)] * len(lead) + [(0, table_rows * width - vec_count * own)]
        return jnp.pad(flat, pad).reshape(lead + (table_rows, width))

    def attn_unfold(full):
        return jnp.moveaxis(full.reshape(grid.devices, -1, own, width), 1, 0).reshape(-1, width, width)

    low = jnp.bfloat16
    first_chunk = jnp.concatenate(
        [fold(attn_weights[:4].astype(low)), fold_table(vectors.astype(low))], 0
    )
    first_full = grid.gather(first_chunk)
    second_full = grid.gather(fold(attn_weights[4:].astype(low)))
    ffn_chunk = jnp.concatenate([ffn_out.astype(low), fold(ffn_in.astype(low))], 0)
    ffn_full = grid.gather(ffn_chunk)
    out_rows = ffn_out.shape[0]
    attn_full = jnp.concatenate([attn_unfold(first_full[..., : 4 * own, :]), attn_unfold(second_full)])
    ffn_out_full = ffn_full[..., :out_rows, :].reshape(-1, width)
    ffn_in_full = ffn_full[..., out_rows:, :].reshape(width, -1)
    table_full = first_full[..., 4 * own :, :].reshape(grid.devices, table_rows * width)
    table_full = table_full[:, : vec_count * own].reshape(grid.devices, vec_count, own)
    table_full = jnp.moveaxis(table_full, 1, 0).reshape(vec_count, width)
    attn_back, ffn_in_back, ffn_out_back = attn_full, ffn_in_full, ffn_out_full
    table = table_full.astype(jnp.float32)
    seqs, length, width = inputs.shape
    mem_len = memory.shape[1]
    tokens = seqs * length
    positions = jnp.arange(length)
    valid = positions[None, :] < lengths[:, None]
    self_mask = (positions[:, None] >= positions[None, :])[None, None] & valid[:, None, None, :]
    cross_mask = (jnp.arange(mem_len)[None, :] < mem_lengths[:, None])[:, None, None, :]

    def split_heads(flat, rows):
        return flat.reshape(seqs, rows, HEADS, HEAD_DIM)

    def join_heads(grid):
        return grid.reshape(-1, width)

    resid = inputs.astype(jnp.float32).reshape(tokens, width)
    mem_flat = memory.reshape(seqs * mem_len, width)
    normed_one, norm_one_back = jax.vjp(layer_norm, resid, table[0], table[1])
    act_one = normed_one.astype(jnp.bfloat16)
    query_self = (plain_dot(act_one, attn_full[0]) + table[6]).astype(jnp.bfloat16)
    key_self = plain_dot(act_one, attn_full[1]).astype(jnp.bfloat16)
    value_self = (plain_dot(act_one, attn_full[2]) + table[7]).astype(jnp.bfloat16)
    mixed_self, logsum_self = attend_forward(
        split_heads(query_self, length),
        split_heads(key_self, length),
        split_heads(value_self, length),
        self_mask,
    )
    mixed_self = join_heads(mixed_self).astype(jnp.bfloat16)
    resid_one = resid + plain_dot(mixed_self, attn_full[3]) + table[8]
    normed_two, norm_two_back = jax.vjp(layer_norm, resid_one, table[2], table[3])
    act_two = normed_two.astype(jnp.bfloat16)
    query_cross = (plain_dot(act_two, attn_full[4]) + table[9]).astype(jnp.bfloat16)
    key_cross = plain_dot(mem_flat, attn_full[5]).astype(jnp.bfloat16)
    value_cross = (plain_dot(mem_flat, attn_full[6]) + table[10]).astype(jnp.bfloat16)
    mixed_cross, logsum_cross = attend_forward(
        split_heads(query_cross, length),
        split_heads(key_cross, mem_len),
        split_heads(value_cross, mem_len),
        cross_mask,
    )
    mixed_cross = join_heads(mixed_cross).astype(jnp.bfloat16)
    resid_two = resid_one + plain_dot(mixed_cross, attn_full[7]) + table[11]
    normed_three, norm_three_back = jax.vjp(layer_norm, resid_two, table[4], table[5])
    act_three = normed_three.astype(jnp.bfloat16)
    hidden_pre = plain_dot(act_three, ffn_in_full) + table[13:].reshape(-1)
    hidden, gelu_back = jax.vjp(partial(jax.nn.gelu, approximate=False), hidden_pre)
    hidden_low = hidden.astype(jnp.bfloat16)
    output = resid_two + plain_dot(hidden_low, ffn_out_full) + table[12]
    grad_out = cotangent.astype(jnp.float32).reshape(tokens, width) * valid.reshape(tokens)[
        :, None
    ].astype(jnp.float32)
    grad_branch = grad_out.astype(jnp.bfloat16)
    grad_ffn_out = left_dot(hidden_low, grad_branch)
    grad_out_bias = column_sum(grad_branch)
    grad_hidden = right_dot(grad_branch, ffn_out_back)
    grad_pre = gelu_back(grad_hidden)[0].astype(jnp.bfloat16)
    grad_ffn_in = left_dot(act_three, grad_pre)
    grad_in_bias = column_sum(grad_pre)
    back_three = norm_three_back(right_dot(grad_pre, ffn_in_back))
    grad_two = grad_out + back_three[0]
    branch_two = grad_two.astype(jnp.bfloat16)
    grad_wo_cross = left_dot(mixed_cross, branch_two)
    grad_bo_cross = column_sum(branch_two)
    grad_mixed_cross = right_dot(branch_two, attn_back[7]).astype(jnp.bfloat16)
    cross_grads = attend_backward(
        split_heads(query_cross, length),
        split_heads(key_cross, mem_len),
        split_heads(value_cross, mem_len),
        cross_mask,
        logsum_cross,
        split_heads(grad_mixed_cross, length),
    )
    grad_query_cross = join_heads(cross_grads[0]).astype(jnp.bfloat16)
    grad_key_cross = join_heads(cross_grads[1]).astype(jnp.bfloat16)
    grad_value_cross = join_heads(cross_grads[2]).astype(jnp.bfloat16)
    grad_wq_cross = left_dot(act_two, grad_query_cross)
    grad_bq_cross = column_sum(grad_query_cross)
    grad_wk_cross = left_dot(mem_flat, grad_key_cross)
    grad_wv_cross = left_dot(mem_flat, grad_value_cross)
    grad_bv_cross = column_sum(grad_value_cross)
    grad_memory = right_dot(grad_key_cross, attn_back[5]) + right_dot(
        grad_value_cross, attn_back[6]
    )
    back_two = norm_two_back(right_dot(grad_query_cross, attn_back[4]))
    grad_one = grad_two + back_two[0]
    grad_cross_stack = jnp.stack([grad_wq_cross, grad_wk_cross, grad_wv_cross, grad_wo_cross])
    branch_one = grad_one.astype(jnp.bfloat16)
    grad_wo_self = left_dot(mixed_self, branch_one)
    grad_bo_self = column_sum(branch_one)
    grad_mixed_self = right_dot(branch_one, attn_back[3]).astype(jnp.bfloat16)
    self_grads = attend_backward(
        split_heads(query_self, length),
        split_heads(key_self, length),
        split_heads(value_self, length),
        self_mask,
        logsum_self,
        split_heads(grad_mixed_self, length),
    )
    grad_query_self = join_heads(self_grads[0]).astype(jnp.bfloat16)
    grad_key_self = join_heads(self_grads[1]).astype(jnp.bfloat16)
    grad_value_self = join_heads(self_grads[2]).astype(jnp.bfloat16)
    grad_wq_self = left_dot(act_one, grad_query_self)
    grad_wk_self = left_dot(act_one, grad_key_self)
    grad_wv_self = left_dot(act_one, grad_value_self)
    grad_bq_self = column_sum(grad_query_self)
    grad_bv_self = column_sum(grad_value_self)
    grad_act_one = (
        right_dot(grad_query_self, attn_back[0])
        + right_dot(grad_key_self, attn_back[1])
        + right_dot(grad_value_self, attn_back[2])
    )
    back_one = norm_one_back(grad_act_one)
    grad_input = grad_one + back_one[0]
    grad_self_stack = jnp.stack([grad_wq_self, grad_wk_self, grad_wv_self, grad_wo_self])
    small_rows = jnp.stack(
        [
            back_one[1],
            back_one[2],
            back_two[1],
            back_two[2],
            back_three[1],
            back_three[2],
            grad_bq_self,
            grad_bv_self,
            grad_bo_self,
            grad_bq_cross,
            grad_bv_cross,
            grad_bo_cross,
            grad_out_bias,
        ]
    )
    grad_table = jnp.concatenate([small_rows, grad_in_bias.reshape(-1, width)], 0)

    def attn_fold(stack):
        parts = stack.reshape(4, grid.devices, own, width)
        return jnp.moveaxis(parts, 0, 1).reshape(grid.devices, 4 * own, width)

    grad_parts = jnp.moveaxis(grad_table.reshape(vec_count, grid.devices, own), 0, 1)
    last_parts = jnp.concatenate(
        [attn_fold(grad_self_stack), fold_table(grad_parts, (grid.devices,))], 1
    )
    ffn_parts = jnp.concatenate(
        [
            grad_ffn_out.reshape(grid.devices, -1, width),
            grad_ffn_in.reshape(grid.devices, -1, width),
        ],
        1,
    )

    def reduce(parts):
        return grid.scatter(parts.reshape(spots + parts.shape[1:]))

    ffn_share = reduce(ffn_parts)
    cross_share = reduce(attn_fold(grad_cross_stack))
    last_share = reduce(last_parts)
    self_share = last_share[: 4 * own].reshape(4, own, width)
    table_share = last_share[4 * own :].reshape(-1)[: vec_count * own].reshape(vec_count, own)
    shares = (
        jnp.concatenate([self_share, cross_share.reshape(4, own, width)], 0),
        ffn_share[out_rows:].reshape(ffn_in.shape),
        ffn_share[:out_rows],
        table_share,
    )
    local_squares = (
        jnp.sum(shares[0] * shares[0])
        + jnp.sum(shares[1] * shares[1])
        + jnp.sum(shares[2] * shares[2])
        + jnp.sum(shares[3] * shares[3])
    )
    spread = jnp.broadcast_to(local_squares, (grid.devices, 8, 128))
    total_squares = jnp.sum(lax.all_to_all(spread, AXES, 0, 0)[:, 0, 0])
    grad_norm = jnp.sqrt(total_squares)
    clip_scale = jnp.minimum(1.0, 1.0 / (grad_norm + 1e-06))
    step = jnp.float32(STEP)
    attn_new = adam_update(attn_weights, shares[0], attn_first, attn_second, clip_scale, step, 0.04)
    first_new = adam_update(ffn_in, shares[1], ffn_in_first, ffn_in_second, clip_scale, step, 0.04)
    second_new = adam_update(
        ffn_out, shares[2], ffn_out_first, ffn_out_second, clip_scale, step, 0.04
    )
    table_new = adam_update(vectors, shares[3], vector_first, vector_second, clip_scale, step, 0.25)
    return (
        output.reshape(seqs, length, width),
        grad_input.reshape(seqs, length, width),
        grad_memory.reshape(seqs, mem_len, width),
        grad_norm.reshape(1),
        attn_new[0],
        attn_new[1],
        attn_new[2],
        first_new[0],
        first_new[1],
        first_new[2],
        second_new[0],
        second_new[1],
        second_new[2],
        table_new[0],
        table_new[1],
        table_new[2],
    )


def solution(mesh):
    def whole(*arrays):
        return local(Grid(mesh.shape["dp"], mesh.shape["fsdp"]), *arrays)

    return jax.shard_map(
        whole,
        mesh=mesh,
        in_specs=(
            P(("dp", "fsdp"), None, None),
            P(("dp", "fsdp"), None, None),
            P(("dp", "fsdp"), None, None),
            P(("dp", "fsdp")),
            P(("dp", "fsdp")),
            P(None, ("dp", "fsdp"), None),
            P(("dp", "fsdp"), None),
            P(("dp", "fsdp"), None),
            P(None, ("dp", "fsdp")),
            P(None, ("dp", "fsdp"), None),
            P(None, ("dp", "fsdp"), None),
            P(("dp", "fsdp"), None),
            P(("dp", "fsdp"), None),
            P(("dp", "fsdp"), None),
            P(("dp", "fsdp"), None),
            P(None, ("dp", "fsdp")),
            P(None, ("dp", "fsdp")),
        ),
        out_specs=(
            P(("dp", "fsdp"), None, None),
            P(("dp", "fsdp"), None, None),
            P(("dp", "fsdp"), None, None),
            P(),
            P(None, ("dp", "fsdp"), None),
            P(None, ("dp", "fsdp"), None),
            P(None, ("dp", "fsdp"), None),
            P(("dp", "fsdp"), None),
            P(("dp", "fsdp"), None),
            P(("dp", "fsdp"), None),
            P(("dp", "fsdp"), None),
            P(("dp", "fsdp"), None),
            P(("dp", "fsdp"), None),
            P(None, ("dp", "fsdp")),
            P(None, ("dp", "fsdp")),
            P(None, ("dp", "fsdp")),
        ),
        check_vma=False,
    )
```

```python
import jax
import jax.numpy as jnp
from jax import lax
from jax.experimental import pallas as pl
from jax.experimental.pallas import tpu as pltpu
from jax.sharding import PartitionSpec as P

HEADS = 8
HEAD_DIM = 64
STEP = 5
PAIR = 2 * HEAD_DIM
SCALE = HEAD_DIM ** (-0.5)
LOW = jnp.bfloat16
F32 = jnp.float32
LIMIT = 60 * 1024 * 1024


def dot_nn(left, right):
    return lax.dot_general(left, right, (((1,), (0,)), ((), ())), preferred_element_type=F32)


def dot_nt(left, right):
    return lax.dot_general(left, right, (((1,), (1,)), ((), ())), preferred_element_type=F32)


def dot_tn(left, right):
    return lax.dot_general(left, right, (((0,), (0,)), ((), ())), preferred_element_type=F32)


def normalize(values):
    center = values - jnp.mean(values, -1, keepdims=True)
    inverse = lax.rsqrt(jnp.mean(center * center, -1, keepdims=True) + 1e-05)
    return center * inverse, inverse


def normalize_back(grad, hat, inverse, gain):
    grad_hat = grad * (1.0 + gain)
    first = jnp.mean(grad_hat, -1, keepdims=True)
    second = jnp.mean(grad_hat * hat, -1, keepdims=True)
    return inverse * (grad_hat - first - hat * second)


def column_sum(values):
    return jnp.sum(values.astype(F32), 0, keepdims=True)


def half_of(pair, odd):
    lane = lax.broadcasted_iota(jnp.int32, pair.shape, 1)
    keep = lane >= HEAD_DIM if odd else lane < HEAD_DIM
    return jnp.where(keep, pair, jnp.zeros_like(pair))


def self_bias(size, count):
    key = lax.broadcasted_iota(jnp.int32, (size, size), 0)
    query = lax.broadcasted_iota(jnp.int32, (size, size), 1)
    return jnp.where((key <= query) & (key < count), 0.0, -1e30)


def cross_bias(keys, queries, count):
    key = lax.broadcasted_iota(jnp.int32, (keys, queries), 0)
    return jnp.where(key < count, 0.0, -1e30)


def attend(query, key, value, bias_ref, mixed_ref, lse_ref):
    value_t = value.T
    for pair in range(HEADS // 2):
        cols = slice(pair * PAIR, (pair + 1) * PAIR)
        query_pair, key_pair = query[:, cols] * SCALE, key[:, cols]
        for odd in range(2):
            head = 2 * pair + odd
            rows = slice(head * HEAD_DIM, (head + 1) * HEAD_DIM)
            scores = dot_nt(half_of(key_pair, odd), query_pair) + bias_ref[...]
            top = jnp.max(scores, 0, keepdims=True)
            expo = jnp.exp(scores - top)
            total = jnp.sum(expo, 0, keepdims=True)
            probs = (expo * (1.0 / total)).astype(LOW)
            mixed_ref[rows] = dot_nn(value_t[rows], probs)
            lse_ref[0, head : head + 1] = top + jnp.log(total)


def attend_back(query_ref, key_ref, value_ref, grad, bias_ref, lse_ref, gq_ref, gk_ref, gv_ref):
    key_t = key_ref[0].T
    for pair in range(HEADS // 2):
        cols = slice(pair * PAIR, (pair + 1) * PAIR)
        query_pair = query_ref[0, :, cols] * SCALE
        key_pair, value_pair, grad_pair = key_ref[0, :, cols], value_ref[0, :, cols], grad[:, cols]
        grad_key = grad_value = None
        for odd in range(2):
            head = 2 * pair + odd
            rows = slice(head * HEAD_DIM, (head + 1) * HEAD_DIM)
            scores = dot_nt(half_of(key_pair, odd), query_pair) + bias_ref[...]
            probs = jnp.exp(scores - lse_ref[0, head : head + 1])
            grad_probs = dot_nt(half_of(value_pair, odd), grad_pair)
            inner = jnp.sum(probs * grad_probs, 0, keepdims=True)
            grad_scores = (probs * (grad_probs - inner)).astype(LOW)
            to_value = dot_nn(probs.astype(LOW), half_of(grad_pair, odd))
            to_key = dot_nn(grad_scores, half_of(query_pair, odd))
            grad_value = to_value if grad_value is None else grad_value + to_value
            grad_key = to_key if grad_key is None else grad_key + to_key
            gq_ref[rows] = dot_nn(key_t[rows], grad_scores)
        gk_ref[:, cols] = grad_key.astype(LOW)
        gv_ref[:, cols] = grad_value.astype(LOW)


def self_forward_kernel(
    count_ref, x_ref, w_ref, table_ref,
    act_ref, query_ref, key_ref, value_ref, mixed_ref, lse_ref, out_ref,
    bias, mixed_t,
):
    bias[...] = self_bias(bias.shape[0], count_ref[pl.program_id(0)])
    x = x_ref[0].astype(F32)
    hat, _ = normalize(x)
    act = (hat * (1.0 + table_ref[0:1]) + table_ref[1:2]).astype(LOW)
    act_ref[0] = act
    query = (dot_nn(act, w_ref[0]) + table_ref[6:7]).astype(LOW)
    key = dot_nn(act, w_ref[1]).astype(LOW)
    value = (dot_nn(act, w_ref[2]) + table_ref[7:8]).astype(LOW)
    query_ref[0], key_ref[0], value_ref[0] = query, key, value
    attend(query, key, value, bias, mixed_t, lse_ref)
    mixed = mixed_t[...].T.astype(LOW)
    mixed_ref[0] = mixed
    out_ref[0] = x + dot_nn(mixed, w_ref[3]) + table_ref[8:9]


def cross_forward_kernel(
    count_ref, x_ref, mem_ref, w_ref, table_ref,
    act_ref, query_ref, key_ref, value_ref, mixed_ref, lse_ref, out_ref,
    bias, mixed_t,
):
    bias[...] = cross_bias(*bias.shape, count_ref[pl.program_id(0)])
    x = x_ref[0]
    hat, _ = normalize(x)
    act = (hat * (1.0 + table_ref[2:3]) + table_ref[3:4]).astype(LOW)
    act_ref[0] = act
    query = (dot_nn(act, w_ref[0]) + table_ref[9:10]).astype(LOW)
    key = dot_nn(mem_ref[0], w_ref[1]).astype(LOW)
    value = (dot_nn(mem_ref[0], w_ref[2]) + table_ref[10:11]).astype(LOW)
    query_ref[0], key_ref[0], value_ref[0] = query, key, value
    attend(query, key, value, bias, mixed_t, lse_ref)
    mixed = mixed_t[...].T.astype(LOW)
    mixed_ref[0] = mixed
    out_ref[0] = x + dot_nn(mixed, w_ref[3]) + table_ref[11:12]


def ffn_kernel(
    count_ref, x_ref, cot_ref, w_in_ref, w_out_ref, table_ref, bias_ref,
    out_ref, grad_ref, gw_in_ref, gw_out_ref, gb_in_ref, small_ref,
    act, gf, hidden, gpre, back,
):
    step = pl.program_id(0)
    seqs, length, width = x_ref.shape

    def valid(seq):
        row = lax.broadcasted_iota(jnp.int32, (length, 1), 0)
        return (row < count_ref[seq]).astype(F32)

    @pl.when(step == 0)
    def _():
        small_ref[...] = jnp.zeros_like(small_ref)
        for seq in range(seqs):
            x = x_ref[seq]
            hat, _ = normalize(x)
            act[seq] = (hat * (1.0 + table_ref[4:5]) + table_ref[5:6]).astype(LOW)
            grad = (cot_ref[seq].astype(F32) * valid(seq)).astype(LOW)
            gf[seq] = grad
            small_ref[2:3] += column_sum(grad)
            out_ref[seq] = x + table_ref[12:13]
            back[seq] = jnp.zeros_like(back[seq])

    sums = jnp.zeros((1, w_in_ref.shape[1]), F32)
    for seq in range(seqs):
        pre = dot_nn(act[seq], w_in_ref[...]) + bias_ref[...]
        cdf = 0.5 + 0.5 * lax.erf(pre * 0.5**0.5)
        slope = cdf + pre * (jnp.exp(pre * pre * -0.5) * 0.3989422804014327)
        unit = (pre * cdf).astype(LOW)
        hidden[seq] = unit
        grad_pre = (dot_nt(gf[seq], w_out_ref[...]) * slope).astype(LOW)
        gpre[seq] = grad_pre
        sums += column_sum(grad_pre)
        out_ref[seq] += dot_nn(unit, w_out_ref[...])
        back[seq] += dot_nt(grad_pre, w_in_ref[...])
    gb_in_ref[...] = sums
    tokens = seqs * length
    hidden_all, gf_all = hidden[...].reshape(tokens, -1), gf[...].reshape(tokens, -1)
    act_all, gpre_all = act[...].reshape(tokens, -1), gpre[...].reshape(tokens, -1)
    gw_out_ref[...] = dot_tn(hidden_all, gf_all).astype(gw_out_ref.dtype)
    gw_in_ref[...] = dot_tn(act_all, gpre_all).astype(gw_in_ref.dtype)

    @pl.when(step == pl.num_programs(0) - 1)
    def _():
        for seq in range(seqs):
            hat, inverse = normalize(x_ref[seq])
            grad = back[seq]
            small_ref[0:1] += column_sum(grad * hat)
            small_ref[1:2] += column_sum(grad)
            grad_ref[seq] = cot_ref[seq].astype(F32) * valid(seq) + normalize_back(
                grad, hat, inverse, table_ref[4:5]
            )


def cross_back_kernel(
    count_ref, grad_ref, x_ref, act_ref, mem_ref, query_ref, key_ref, value_ref, mixed_ref, lse_ref,
    w_ref, table_ref,
    out_ref, gmem_ref, gw_ref, small_ref,
    bias, gq_t, gk, gv,
):
    step = pl.program_id(0)

    @pl.when(step == 0)
    def _():
        gw_ref[...] = jnp.zeros_like(gw_ref)
        small_ref[...] = jnp.zeros_like(small_ref)

    bias[...] = cross_bias(*bias.shape, count_ref[step])
    grad = grad_ref[0]
    low = grad.astype(LOW)
    gw_ref[3] += dot_tn(mixed_ref[0], low)
    small_ref[4:5] += column_sum(low)
    grad_mixed = dot_nt(low, w_ref[3]).astype(LOW)
    attend_back(query_ref, key_ref, value_ref, grad_mixed, bias, lse_ref, gq_t, gk, gv)
    gq = (gq_t[...] * SCALE).T.astype(LOW)
    small_ref[2:3] += column_sum(gq)
    small_ref[3:4] += column_sum(gv[...])
    gw_ref[0] += dot_tn(act_ref[0], gq)
    gw_ref[1] += dot_tn(mem_ref[0], gk[...])
    gw_ref[2] += dot_tn(mem_ref[0], gv[...])
    gmem_ref[0] = dot_nt(gk[...], w_ref[1]) + dot_nt(gv[...], w_ref[2])
    back = dot_nt(gq, w_ref[0])
    hat, inverse = normalize(x_ref[0])
    small_ref[0:1] += column_sum(back * hat)
    small_ref[1:2] += column_sum(back)
    out_ref[0] = grad + normalize_back(back, hat, inverse, table_ref[2:3])


def self_back_kernel(
    count_ref, grad_ref, x_ref, act_ref, query_ref, key_ref, value_ref, mixed_ref, lse_ref,
    w_ref, table_ref,
    out_ref, gw_ref, small_ref,
    bias, gq_t, gk, gv,
):
    step = pl.program_id(0)

    @pl.when(step == 0)
    def _():
        gw_ref[...] = jnp.zeros_like(gw_ref)
        small_ref[...] = jnp.zeros_like(small_ref)

    bias[...] = self_bias(bias.shape[0], count_ref[step])
    grad = grad_ref[0]
    low = grad.astype(LOW)
    gw_ref[3] += dot_tn(mixed_ref[0], low)
    small_ref[4:5] += column_sum(low)
    grad_mixed = dot_nt(low, w_ref[3]).astype(LOW)
    attend_back(query_ref, key_ref, value_ref, grad_mixed, bias, lse_ref, gq_t, gk, gv)
    gq = (gq_t[...] * SCALE).T.astype(LOW)
    small_ref[2:3] += column_sum(gq)
    small_ref[3:4] += column_sum(gv[...])
    gw_ref[0] += dot_tn(act_ref[0], gq)
    gw_ref[1] += dot_tn(act_ref[0], gk[...])
    gw_ref[2] += dot_tn(act_ref[0], gv[...])
    back = dot_nt(gq, w_ref[0]) + dot_nt(gk[...], w_ref[1]) + dot_nt(gv[...], w_ref[2])
    hat, inverse = normalize(x_ref[0].astype(F32))
    small_ref[0:1] += column_sum(back * hat)
    small_ref[1:2] += column_sum(back)
    out_ref[0] = grad + normalize_back(back, hat, inverse, table_ref[0:1])


def by_seq(*tail):
    return pl.BlockSpec((1,) + tail, lambda seq, *_: (seq,) + (0,) * len(tail))


def fixed(*shape):
    return pl.BlockSpec(shape, lambda *_: (0,) * len(shape))


def call(kernel, name, grid, counts, args, in_specs, outs, out_specs, scratch):
    return pl.pallas_call(
        kernel,
        out_shape=[jax.ShapeDtypeStruct(*out) for out in outs],
        grid_spec=pltpu.PrefetchScalarGridSpec(
            num_scalar_prefetch=1, grid=grid, in_specs=in_specs, out_specs=out_specs, scratch_shapes=scratch
        ),
        compiler_params=pltpu.CompilerParams(vmem_limit_bytes=LIMIT),
        name=name,
    )(counts, *args)


def self_forward(lengths, x, weights, table):
    seqs, length, width = x.shape
    shape = (seqs, length, width)
    block = by_seq(length, width)
    return call(
        self_forward_kernel, "self_forward", (seqs,), lengths, (x, weights, table),
        [block, fixed(4, width, width), fixed(*table.shape)],
        [(shape, LOW)] * 5 + [((seqs, HEADS, length), F32), (shape, F32)],
        [block] * 5 + [by_seq(HEADS, length), block],
        [pltpu.VMEM((length, length), F32), pltpu.VMEM((width, length), F32)],
    )


def cross_forward(mem_lengths, x, memory, weights, table):
    seqs, length, width = x.shape
    mem_len = memory.shape[1]
    block, mem_block = by_seq(length, width), by_seq(mem_len, width)
    shape, mem_shape = x.shape, memory.shape
    return call(
        cross_forward_kernel, "cross_forward", (seqs,), mem_lengths, (x, memory, weights, table),
        [block, mem_block, fixed(4, width, width), fixed(*table.shape)],
        [(shape, LOW), (shape, LOW), (mem_shape, LOW), (mem_shape, LOW), (shape, LOW), ((seqs, HEADS, length), F32), (shape, F32)],
        [block, block, mem_block, mem_block, block, by_seq(HEADS, length), block],
        [pltpu.VMEM((mem_len, length), F32), pltpu.VMEM((width, length), F32)],
    )


def ffn(lengths, x, cotangent, w_in, w_out, table, grad_type=LOW):
    seqs, length, width = x.shape
    hidden = w_in.shape[1]
    chunk = 512
    bias = table[13:].reshape(1, hidden)
    act = pltpu.VMEM((seqs, length, width), LOW)
    wide = pltpu.VMEM((seqs, length, chunk), LOW)
    cols = pl.BlockSpec((width, chunk), lambda i, *_: (0, i))
    rows = pl.BlockSpec((chunk, width), lambda i, *_: (i, 0))
    flat = pl.BlockSpec((1, chunk), lambda i, *_: (0, i))
    return call(
        ffn_kernel, "ffn", (hidden // chunk,), lengths, (x, cotangent, w_in, w_out, table, bias),
        [fixed(*x.shape), fixed(*x.shape), cols, rows, fixed(*table.shape), flat],
        [(x.shape, F32), (x.shape, F32), (w_in.shape, grad_type), (w_out.shape, grad_type), ((1, hidden), F32), ((8, width), F32)],
        [fixed(*x.shape), fixed(*x.shape), cols, rows, flat, fixed(8, width)],
        [act, act, wide, wide, pltpu.VMEM((seqs, length, width), F32)],
    )


def cross_back(mem_lengths, grad, x, act, memory, query, key, value, mixed, lse, weights, table):
    seqs, length, width = x.shape
    mem_len = memory.shape[1]
    block, mem_block = by_seq(length, width), by_seq(mem_len, width)
    return call(
        cross_back_kernel, "cross_back", (seqs,), mem_lengths,
        (grad, x, act, memory, query, key, value, mixed, lse, weights, table),
        [block, block, block, mem_block, block, mem_block, mem_block, block, by_seq(HEADS, length),
         fixed(4, width, width), fixed(*table.shape)],
        [(x.shape, F32), (memory.shape, F32), (weights.shape, F32), ((8, width), F32)],
        [block, mem_block, fixed(4, width, width), fixed(8, width)],
        [pltpu.VMEM((mem_len, length), F32), pltpu.VMEM((width, length), F32),
         pltpu.VMEM((mem_len, width), LOW), pltpu.VMEM((mem_len, width), LOW)],
    )


def self_back(lengths, grad, x, act, query, key, value, mixed, lse, weights, table):
    seqs, length, width = x.shape
    block = by_seq(length, width)
    return call(
        self_back_kernel, "self_back", (seqs,), lengths,
        (grad, x, act, query, key, value, mixed, lse, weights, table),
        [block] * 7 + [by_seq(HEADS, length), fixed(4, width, width), fixed(*table.shape)],
        [(x.shape, F32), (weights.shape, F32), ((8, width), F32)],
        [block, fixed(4, width, width), fixed(8, width)],
        [pltpu.VMEM((length, length), F32), pltpu.VMEM((width, length), F32),
         pltpu.VMEM((length, width), LOW), pltpu.VMEM((length, width), LOW)],
    )


def adam_update(weight, grad, first, second, clip_scale, step, rate):
    clipped = grad * clip_scale
    first_new = 0.5 * first + 0.5 * clipped
    second_new = 0.55 * second + 0.45 * clipped * clipped
    fix_first = 1.0 - jnp.power(0.5, step)
    fix_second = 1.0 - jnp.power(0.55, step)
    weight_new = weight - rate * (
        first_new / fix_first / (jnp.sqrt(second_new / fix_second) + 1e-08) + 0.01 * weight
    )
    return (weight_new, first_new, second_new)


AXES = ("dp", "fsdp")


class Grid:
    def __init__(self, dp, fsdp):
        self.sizes = (dp, fsdp // 2, 2)
        self.strides = (fsdp, 2, 1)
        self.devices = dp * fsdp
        index = lax.axis_index("fsdp")
        self.place = (lax.axis_index("dp"), index // 2, index % 2)

    def swap(self, values, stage, step):
        stride = self.strides[stage]
        pairs = [(i, i ^ (step * stride)) for i in range(self.devices)]
        return lax.ppermute(values, AXES, pairs)

    def gather(self, chunk):
        held = chunk
        for stage in range(3):
            size, place = self.sizes[stage], self.place[stage]
            parts = [held] + [self.swap(held, stage, step) for step in range(1, size)]
            if size == 2:
                first = jnp.where(place == 0, parts[0], parts[1])
                second = jnp.where(place == 0, parts[1], parts[0])
                held = jnp.stack([first, second], stage)
            else:
                whole = jnp.zeros(held.shape[:stage] + (size,) + held.shape[stage:], held.dtype)
                for step in range(size):
                    whole = lax.dynamic_update_index_in_dim(whole, parts[step], place ^ step, stage)
                held = whole
        return held

    def scatter(self, parts):
        held = parts
        for stage in (2, 1, 0):
            size, place = self.sizes[stage], self.place[stage]
            total = lax.dynamic_index_in_dim(held, place, stage, False).astype(jnp.float32)
            for step in range(1, size):
                piece = lax.dynamic_index_in_dim(held, place ^ step, stage, False)
                total = total + self.swap(piece.astype(jnp.bfloat16), stage, step).astype(jnp.float32)
            held = total
        return held


def local(
    grid,
    inputs,
    memory,
    cotangent,
    lengths,
    mem_lengths,
    attn_weights,
    ffn_in,
    ffn_out,
    vectors,
    attn_first,
    attn_second,
    ffn_in_first,
    ffn_in_second,
    ffn_out_first,
    ffn_out_second,
    vector_first,
    vector_second,
):
    width = inputs.shape[2]
    own = attn_weights.shape[1]
    spots = grid.sizes

    def fold(array):
        return array.reshape(-1, width)

    vec_count = vectors.shape[0]
    table_rows = -(-vec_count * own // width)

    def fold_table(array, lead=()):
        flat = array.reshape(lead + (vec_count * own,))
        pad = [(0, 0)] * len(lead) + [(0, table_rows * width - vec_count * own)]
        return jnp.pad(flat, pad).reshape(lead + (table_rows, width))

    def attn_unfold(full):
        return jnp.moveaxis(full.reshape(grid.devices, -1, own, width), 1, 0).reshape(-1, width, width)

    low = jnp.bfloat16
    first_chunk = jnp.concatenate(
        [fold(attn_weights[:4].astype(low)), fold_table(vectors.astype(low))], 0
    )
    first_full = grid.gather(first_chunk)
    second_full = grid.gather(fold(attn_weights[4:].astype(low)))
    ffn_chunk = jnp.concatenate([ffn_out.astype(low), fold(ffn_in.astype(low))], 0)
    ffn_full = grid.gather(ffn_chunk)
    out_rows = ffn_out.shape[0]
    self_full = attn_unfold(first_full[..., : 4 * own, :])
    cross_full = attn_unfold(second_full)
    ffn_out_full = ffn_full[..., :out_rows, :].reshape(-1, width)
    ffn_in_full = ffn_full[..., out_rows:, :].reshape(width, -1)
    table_full = first_full[..., 4 * own :, :].reshape(grid.devices, table_rows * width)
    table_full = table_full[:, : vec_count * own].reshape(grid.devices, vec_count, own)
    table_full = jnp.moveaxis(table_full, 1, 0).reshape(vec_count, width)
    table = table_full.astype(jnp.float32)
    act_one, query_one, key_one, value_one, mixed_one, lse_one, resid_one = self_forward(
        lengths, inputs, self_full, table
    )
    act_two, query_two, key_two, value_two, mixed_two, lse_two, resid_two = cross_forward(
        mem_lengths, resid_one, memory, cross_full, table
    )
    output, grad_two, grad_ffn_in, grad_ffn_out, grad_in_bias, small_three = ffn(
        lengths, resid_two, cotangent, ffn_in_full, ffn_out_full, table
    )
    grad_one, grad_memory, grad_cross_stack, small_two = cross_back(
        mem_lengths, grad_two, resid_one, act_two, memory, query_two, key_two, value_two, mixed_two,
        lse_two, cross_full, table,
    )
    grad_input, grad_self_stack, small_one = self_back(
        lengths, grad_one, inputs, act_one, query_one, key_one, value_one, mixed_one, lse_one,
        self_full, table,
    )
    grad_table = jnp.concatenate(
        [
            small_one[0:2],
            small_two[0:2],
            small_three[0:2],
            small_one[2:5],
            small_two[2:5],
            small_three[2:3],
            grad_in_bias.reshape(-1, width),
        ],
        0,
    )

    def attn_fold(stack):
        parts = stack.reshape(4, grid.devices, own, width)
        return jnp.moveaxis(parts, 0, 1).reshape(grid.devices, 4 * own, width)

    grad_parts = jnp.moveaxis(grad_table.reshape(vec_count, grid.devices, own), 0, 1)
    last_parts = jnp.concatenate(
        [attn_fold(grad_self_stack), fold_table(grad_parts, (grid.devices,))], 1
    )
    ffn_parts = jnp.concatenate(
        [
            grad_ffn_out.reshape(grid.devices, -1, width),
            grad_ffn_in.reshape(grid.devices, -1, width),
        ],
        1,
    )

    def reduce(parts):
        return grid.scatter(parts.reshape(spots + parts.shape[1:]))

    ffn_share = reduce(ffn_parts)
    cross_share = reduce(attn_fold(grad_cross_stack))
    last_share = reduce(last_parts)
    self_share = last_share[: 4 * own].reshape(4, own, width)
    table_share = last_share[4 * own :].reshape(-1)[: vec_count * own].reshape(vec_count, own)
    shares = (
        jnp.concatenate([self_share, cross_share.reshape(4, own, width)], 0),
        ffn_share[out_rows:].reshape(ffn_in.shape),
        ffn_share[:out_rows],
        table_share,
    )
    local_squares = (
        jnp.sum(shares[0] * shares[0])
        + jnp.sum(shares[1] * shares[1])
        + jnp.sum(shares[2] * shares[2])
        + jnp.sum(shares[3] * shares[3])
    )
    spread = jnp.broadcast_to(local_squares, (grid.devices, 8, 128))
    total_squares = jnp.sum(lax.all_to_all(spread, AXES, 0, 0)[:, 0, 0])
    grad_norm = jnp.sqrt(total_squares)
    clip_scale = jnp.minimum(1.0, 1.0 / (grad_norm + 1e-06))
    step = jnp.float32(STEP)
    attn_new = adam_update(attn_weights, shares[0], attn_first, attn_second, clip_scale, step, 0.04)
    first_new = adam_update(ffn_in, shares[1], ffn_in_first, ffn_in_second, clip_scale, step, 0.04)
    second_new = adam_update(
        ffn_out, shares[2], ffn_out_first, ffn_out_second, clip_scale, step, 0.04
    )
    table_new = adam_update(vectors, shares[3], vector_first, vector_second, clip_scale, step, 0.25)
    return (
        output,
        grad_input,
        grad_memory,
        grad_norm.reshape(1),
        attn_new[0],
        attn_new[1],
        attn_new[2],
        first_new[0],
        first_new[1],
        first_new[2],
        second_new[0],
        second_new[1],
        second_new[2],
        table_new[0],
        table_new[1],
        table_new[2],
    )


def solution(mesh):
    def whole(*arrays):
        return local(Grid(mesh.shape["dp"], mesh.shape["fsdp"]), *arrays)

    return jax.shard_map(
        whole,
        mesh=mesh,
        in_specs=(
            P(("dp", "fsdp"), None, None),
            P(("dp", "fsdp"), None, None),
            P(("dp", "fsdp"), None, None),
            P(("dp", "fsdp")),
            P(("dp", "fsdp")),
            P(None, ("dp", "fsdp"), None),
            P(("dp", "fsdp"), None),
            P(("dp", "fsdp"), None),
            P(None, ("dp", "fsdp")),
            P(None, ("dp", "fsdp"), None),
            P(None, ("dp", "fsdp"), None),
            P(("dp", "fsdp"), None),
            P(("dp", "fsdp"), None),
            P(("dp", "fsdp"), None),
            P(("dp", "fsdp"), None),
            P(None, ("dp", "fsdp")),
            P(None, ("dp", "fsdp")),
        ),
        out_specs=(
            P(("dp", "fsdp"), None, None),
            P(("dp", "fsdp"), None, None),
            P(("dp", "fsdp"), None, None),
            P(),
            P(None, ("dp", "fsdp"), None),
            P(None, ("dp", "fsdp"), None),
            P(None, ("dp", "fsdp"), None),
            P(("dp", "fsdp"), None),
            P(("dp", "fsdp"), None),
            P(("dp", "fsdp"), None),
            P(("dp", "fsdp"), None),
            P(("dp", "fsdp"), None),
            P(("dp", "fsdp"), None),
            P(None, ("dp", "fsdp")),
            P(None, ("dp", "fsdp")),
            P(None, ("dp", "fsdp")),
        ),
        check_vma=False,
    )
```

```python
from functools import partial

import jax
import jax.numpy as jnp
from jax import lax
from jax.experimental import pallas as pl
from jax.experimental.pallas import tpu as pltpu
from jax.sharding import PartitionSpec as P

HEADS = 8
HEAD_DIM = 64
STEP = 5
AXES = ("dp", "fsdp")
PAIR = 2 * HEAD_DIM
SCALE = HEAD_DIM ** (-0.5)
LOW = jnp.bfloat16
F32 = jnp.float32
LIMIT = 60 * 1024 * 1024


def dot_nn(left, right):
    return lax.dot_general(left, right, (((1,), (0,)), ((), ())), preferred_element_type=F32)


def dot_nt(left, right):
    return lax.dot_general(left, right, (((1,), (1,)), ((), ())), preferred_element_type=F32)


def dot_tn(left, right):
    return lax.dot_general(left, right, (((0,), (0,)), ((), ())), preferred_element_type=F32)


def normalize(values):
    center = values - jnp.mean(values, -1, keepdims=True)
    inverse = lax.rsqrt(jnp.mean(center * center, -1, keepdims=True) + 1e-05)
    return center * inverse, inverse


def normalize_back(grad, hat, inverse, gain):
    grad_hat = grad * (1.0 + gain)
    first = jnp.mean(grad_hat, -1, keepdims=True)
    second = jnp.mean(grad_hat * hat, -1, keepdims=True)
    return inverse * (grad_hat - first - hat * second)


def column_sum(values):
    return jnp.sum(values.astype(F32), 0, keepdims=True)


def half_of(pair, odd):
    lane = lax.broadcasted_iota(jnp.int32, pair.shape, 1)
    keep = lane >= HEAD_DIM if odd else lane < HEAD_DIM
    return jnp.where(keep, pair, jnp.zeros_like(pair))


def self_bias(size, count):
    key = lax.broadcasted_iota(jnp.int32, (size, size), 0)
    query = lax.broadcasted_iota(jnp.int32, (size, size), 1)
    return jnp.where((key <= query) & (key < count), 0.0, -1e30)


def cross_bias(keys, queries, count):
    key = lax.broadcasted_iota(jnp.int32, (keys, queries), 0)
    return jnp.where(key < count, 0.0, -1e30)


def attend(query, key, value, bias_ref, mixed_ref, lse_ref):
    value_t = value.T
    for pair in range(HEADS // 2):
        cols = slice(pair * PAIR, (pair + 1) * PAIR)
        query_pair, key_pair = query[:, cols] * SCALE, key[:, cols]
        for odd in range(2):
            head = 2 * pair + odd
            rows = slice(head * HEAD_DIM, (head + 1) * HEAD_DIM)
            scores = dot_nt(half_of(key_pair, odd), query_pair) + bias_ref[...]
            top = jnp.max(scores, 0, keepdims=True)
            expo = jnp.exp(scores - top)
            total = jnp.sum(expo, 0, keepdims=True)
            probs = (expo * (1.0 / total)).astype(LOW)
            mixed_ref[rows] = dot_nn(value_t[rows], probs)
            lse_ref[0, head : head + 1] = top + jnp.log(total)


def attend_back(query_ref, key_ref, value_ref, grad, bias_ref, lse_ref, gq_ref, gk_ref, gv_ref):
    key_t = key_ref[0].T
    for pair in range(HEADS // 2):
        cols = slice(pair * PAIR, (pair + 1) * PAIR)
        query_pair = query_ref[0, :, cols] * SCALE
        key_pair, value_pair, grad_pair = key_ref[0, :, cols], value_ref[0, :, cols], grad[:, cols]
        grad_key = grad_value = None
        for odd in range(2):
            head = 2 * pair + odd
            rows = slice(head * HEAD_DIM, (head + 1) * HEAD_DIM)
            scores = dot_nt(half_of(key_pair, odd), query_pair) + bias_ref[...]
            probs = jnp.exp(scores - lse_ref[0, head : head + 1])
            grad_probs = dot_nt(half_of(value_pair, odd), grad_pair)
            inner = jnp.sum(probs * grad_probs, 0, keepdims=True)
            grad_scores = (probs * (grad_probs - inner)).astype(LOW)
            to_value = dot_nn(probs.astype(LOW), half_of(grad_pair, odd))
            to_key = dot_nn(grad_scores, half_of(query_pair, odd))
            grad_value = to_value if grad_value is None else grad_value + to_value
            grad_key = to_key if grad_key is None else grad_key + to_key
            gq_ref[rows] = dot_nn(key_t[rows], grad_scores)
        gk_ref[0, :, cols] = grad_key.astype(LOW)
        gv_ref[0, :, cols] = grad_value.astype(LOW)


def place_weights(place_ref, mine_ref, other_ref, blocks, outs, turned=None, table_ref=None):
    planes, depths = mine_ref.shape[:2]
    for plane in range(planes):
        for depth in range(depths):
            base = ((depth ^ place_ref[0]) * planes + (plane ^ place_ref[1])) * 2
            for ref, core in ((mine_ref, place_ref[2]), (other_ref, 1 - place_ref[2])):
                for out, row, own, col in blocks:
                    first = pl.multiple_of((base + core) * own, own)
                    piece = ref[plane, depth, row : row + own]
                    if isinstance(col, int):
                        outs[out][col, pl.ds(first, own)] = piece
                    else:
                        outs[out][pl.ds(first, own), col] = piece
                if turned is not None:
                    row = blocks[-1][1] + blocks[-1][2]
                    piece = ref[plane, depth, row : row + 8].astype(F32)
                    first = pl.multiple_of((base + core) * 16, 16)
                    turned[pl.ds(first, 8)] = piece[:, :128]
                    turned[pl.ds(pl.multiple_of(first + 8, 8), 8)] = piece[:, 128:256]
    if turned is not None:
        table_ref[...] = turned[...].T[: table_ref.shape[0]]


def attn_blocks(own):
    return [(0, i * own, own, i) for i in range(4)]


def ffn_blocks(own, out_rows, width, blocks):
    spots = [(1, 0, out_rows, slice(None))]
    return spots + [(0, out_rows + i * own, own, slice(i * width, (i + 1) * width)) for i in range(blocks)]


def self_forward_kernel(own, count_ref, place_ref, x_ref, *refs):
    act_ref, query_ref, key_ref, value_ref, mixed_ref, lse_ref, out_ref = refs[2:9]
    if own:
        w_ref, table_ref, bias, mixed_t, turned = refs[9:]

        @pl.when(pl.program_id(0) == 0)
        def _():
            place_weights(place_ref, refs[0], refs[1], attn_blocks(own), (w_ref,), turned, table_ref)
    else:
        w_ref, table_ref = refs[:2]
        bias, mixed_t = refs[9:]
    bias[...] = self_bias(bias.shape[0], count_ref[pl.program_id(0)])
    x = x_ref[0].astype(F32)
    hat, _ = normalize(x)
    act = (hat * (1.0 + table_ref[0:1]) + table_ref[1:2]).astype(LOW)
    act_ref[0] = act
    query = (dot_nn(act, w_ref[0]) + table_ref[6:7]).astype(LOW)
    key = dot_nn(act, w_ref[1]).astype(LOW)
    value = (dot_nn(act, w_ref[2]) + table_ref[7:8]).astype(LOW)
    query_ref[0], key_ref[0], value_ref[0] = query, key, value
    attend(query, key, value, bias, mixed_t, lse_ref)
    mixed = mixed_t[...].T.astype(LOW)
    mixed_ref[0] = mixed
    out_ref[0] = x + dot_nn(mixed, w_ref[3]) + table_ref[8:9]


def cross_forward_kernel(own, count_ref, place_ref, x_ref, mem_ref, table_ref, *refs):
    start = 2 if own else 1
    act_ref, query_ref, key_ref, value_ref, mixed_ref, lse_ref, out_ref = refs[start : start + 7]
    if own:
        w_ref, bias, mixed_t = refs[9:]

        @pl.when(pl.program_id(0) == 0)
        def _():
            place_weights(place_ref, refs[0], refs[1], attn_blocks(own), (w_ref,))
    else:
        w_ref = refs[0]
        bias, mixed_t = refs[8:]
    bias[...] = cross_bias(*bias.shape, count_ref[pl.program_id(0)])
    x = x_ref[0]
    hat, _ = normalize(x)
    act = (hat * (1.0 + table_ref[2:3]) + table_ref[3:4]).astype(LOW)
    act_ref[0] = act
    query = (dot_nn(act, w_ref[0]) + table_ref[9:10]).astype(LOW)
    key = dot_nn(mem_ref[0], w_ref[1]).astype(LOW)
    value = (dot_nn(mem_ref[0], w_ref[2]) + table_ref[10:11]).astype(LOW)
    query_ref[0], key_ref[0], value_ref[0] = query, key, value
    attend(query, key, value, bias, mixed_t, lse_ref)
    mixed = mixed_t[...].T.astype(LOW)
    mixed_ref[0] = mixed
    out_ref[0] = x + dot_nn(mixed, w_ref[3]) + table_ref[11:12]


def emit(place_ref, rows_ref, keep_ref, send_ref, row, own):
    planes, depths = keep_ref.shape[:2]
    for plane in range(planes):
        for depth in range(depths):
            base = ((depth ^ place_ref[0]) * planes + (plane ^ place_ref[1])) * 2
            for ref, core in ((keep_ref, place_ref[2]), (send_ref, 1 - place_ref[2])):
                first = pl.multiple_of((base + core) * own, own)
                ref[plane, depth, row : row + own] = rows_ref[pl.ds(first, own)].astype(ref.dtype)


def ffn_kernel(own, count_ref, place_ref, x_ref, cot_ref, table_ref, bias_ref, *refs):
    step = pl.program_id(0)
    seqs, length, width = x_ref.shape
    out_ref, grad_ref, first_ref, second_ref, small_ref = refs[2:7]
    act, gf, hidden, gpre, back = refs[7:12]
    chunk = hidden.shape[2]
    if own:
        rows, whole_in, whole_out = refs[12:]
        count = first_ref.shape[2]
        w_in_ref = whole_in.at[step]
        w_out_ref = whole_out.at[pl.ds(pl.multiple_of(step * chunk, chunk), chunk)]
    else:
        w_in_ref, w_out_ref = refs[:2]

    def valid(seq):
        row = lax.broadcasted_iota(jnp.int32, (length, 1), 0)
        return (row < count_ref[seq]).astype(F32)

    @pl.when(step == 0)
    def _():
        if own:
            out_rows = count // 2
            spots = [(1, 0, out_rows, slice(None))]
            spots += [(0, out_rows + i * own, own, i) for i in range(whole_in.shape[0])]
            place_weights(place_ref, refs[0], refs[1], spots, (whole_in, whole_out))
        small_ref[...] = jnp.zeros_like(small_ref)
        for seq in range(seqs):
            x = x_ref[seq]
            hat, _ = normalize(x)
            act[seq] = (hat * (1.0 + table_ref[4:5]) + table_ref[5:6]).astype(LOW)
            grad = (cot_ref[seq].astype(F32) * valid(seq)).astype(LOW)
            gf[seq] = grad
            small_ref[2:3] += column_sum(grad)
            out_ref[seq] = x + table_ref[12:13]
            back[seq] = jnp.zeros_like(back[seq])

    sums = jnp.zeros((1, chunk), F32)
    for seq in range(seqs):
        pre = dot_nn(act[seq], w_in_ref[...]) + bias_ref[...]
        cdf = 0.5 + 0.5 * lax.erf(pre * 0.5**0.5)
        slope = cdf + pre * (jnp.exp(pre * pre * -0.5) * 0.3989422804014327)
        unit = (pre * cdf).astype(LOW)
        hidden[seq] = unit
        grad_pre = (dot_nt(gf[seq], w_out_ref[...]) * slope).astype(LOW)
        gpre[seq] = grad_pre
        sums += column_sum(grad_pre)
        out_ref[seq] += dot_nn(unit, w_out_ref[...])
        back[seq] += dot_nt(grad_pre, w_in_ref[...])
    small_ref[pl.ds(8 + step, 1)] = sums
    tokens = seqs * length
    hidden_all, gf_all = hidden[...].reshape(tokens, -1), gf[...].reshape(tokens, -1)
    act_all, gpre_all = act[...].reshape(tokens, -1), gpre[...].reshape(tokens, -1)
    if own:
        planes = first_ref.shape[0]
        rows[...] = dot_tn(act_all, gpre_all)
        for spot in range(4):

            @pl.when(step == spot)
            def _():
                emit(place_ref, rows, first_ref, second_ref, count // 2 + spot * own, own)

        rows[...] = dot_tn(hidden_all, gf_all)
        depth = step ^ place_ref[0]
        for plane in range(planes):
            base = (plane ^ place_ref[1]) * 2
            for ref, core in ((first_ref, place_ref[2]), (second_ref, 1 - place_ref[2])):
                begin = pl.multiple_of((base + core) * (count // 2), count // 2)
                ref[plane, depth, : count // 2] = rows[pl.ds(begin, count // 2)].astype(ref.dtype)
    else:
        first_ref[...] = dot_tn(act_all, gpre_all)
        second_ref[...] = dot_tn(hidden_all, gf_all)

    @pl.when(step == pl.num_programs(0) - 1)
    def _():
        for seq in range(seqs):
            hat, inverse = normalize(x_ref[seq])
            grad = back[seq]
            small_ref[0:1] += column_sum(grad * hat)
            small_ref[1:2] += column_sum(grad)
            grad_ref[seq] = cot_ref[seq].astype(F32) * valid(seq) + normalize_back(
                grad, hat, inverse, table_ref[4:5]
            )


def begin_sums(*refs):
    @pl.when(pl.program_id(0) == 0)
    def _():
        for ref in refs:
            ref[...] = jnp.zeros_like(ref)


def end_sums(own, place_ref, gw, keep_ref, send_ref):
    @pl.when(pl.program_id(0) == pl.num_programs(0) - 1)
    def _():
        for index in range(4):
            emit(place_ref, gw.at[index], keep_ref, send_ref, index * own, own)


def cross_back_kernel(
    own, count_ref, place_ref, grad_ref, x_ref, act_ref, mem_ref, query_ref, key_ref,
    value_ref, mixed_ref, lse_ref, w_ref, table_ref, *refs,
):
    out_ref, gk_ref, gv_ref, small_ref = refs[:4]
    if own:
        keep_ref, send_ref, bias, gq_t, gw = refs[4:]
    else:
        gw, bias, gq_t = refs[4:]
    begin_sums(gw, small_ref)
    bias[...] = cross_bias(*bias.shape, count_ref[pl.program_id(0)])
    grad = grad_ref[0]
    low = grad.astype(LOW)
    gw[3] += dot_tn(mixed_ref[0], low)
    small_ref[4:5] += column_sum(low)
    grad_mixed = dot_nt(low, w_ref[3]).astype(LOW)
    attend_back(query_ref, key_ref, value_ref, grad_mixed, bias, lse_ref, gq_t, gk_ref, gv_ref)
    gq = (gq_t[...] * SCALE).T.astype(LOW)
    small_ref[2:3] += column_sum(gq)
    small_ref[3:4] += column_sum(gv_ref[0])
    gw[0] += dot_tn(act_ref[0], gq)
    gw[1] += dot_tn(mem_ref[0], gk_ref[0])
    gw[2] += dot_tn(mem_ref[0], gv_ref[0])
    back = dot_nt(gq, w_ref[0])
    hat, inverse = normalize(x_ref[0])
    small_ref[0:1] += column_sum(back * hat)
    small_ref[1:2] += column_sum(back)
    out_ref[0] = grad + normalize_back(back, hat, inverse, table_ref[2:3])
    if own:
        end_sums(own, place_ref, gw, keep_ref, send_ref)


def self_back_kernel(
    own, count_ref, place_ref, grad_ref, act_ref, query_ref, key_ref, value_ref, mixed_ref,
    lse_ref, w_ref, *refs,
):
    gq_ref, gk_ref, gv_ref, small_ref = refs[:4]
    if own:
        keep_ref, send_ref, bias, gq_t, gw = refs[4:]
    else:
        gw, bias, gq_t = refs[4:]
    begin_sums(gw, small_ref)
    bias[...] = self_bias(bias.shape[0], count_ref[pl.program_id(0)])
    low = grad_ref[0].astype(LOW)
    gw[3] += dot_tn(mixed_ref[0], low)
    small_ref[4:5] += column_sum(low)
    grad_mixed = dot_nt(low, w_ref[3]).astype(LOW)
    attend_back(query_ref, key_ref, value_ref, grad_mixed, bias, lse_ref, gq_t, gk_ref, gv_ref)
    gq = (gq_t[...] * SCALE).T.astype(LOW)
    gq_ref[0] = gq
    small_ref[2:3] += column_sum(gq)
    small_ref[3:4] += column_sum(gv_ref[0])
    gw[0] += dot_tn(act_ref[0], gq)
    gw[1] += dot_tn(act_ref[0], gk_ref[0])
    gw[2] += dot_tn(act_ref[0], gv_ref[0])
    if own:
        end_sums(own, place_ref, gw, keep_ref, send_ref)


def memory_kernel(gk_ref, gv_ref, w_ref, out_ref):
    out_ref[0] = dot_nt(gk_ref[0], w_ref[1]) + dot_nt(gv_ref[0], w_ref[2])


def input_kernel(own, place_ref, grad_ref, x_ref, gq_ref, gk_ref, gv_ref, w_ref, table_ref, *refs):
    out_ref, small_ref = refs[-4:-2] if own else refs[-2:]
    begin_sums(small_ref)
    back = dot_nt(gq_ref[0], w_ref[0]) + dot_nt(gk_ref[0], w_ref[1]) + dot_nt(gv_ref[0], w_ref[2])
    hat, inverse = normalize(x_ref[0].astype(F32))
    small_ref[0:1] += column_sum(back * hat)
    small_ref[1:2] += column_sum(back)
    out_ref[0] = grad_ref[0] + normalize_back(back, hat, inverse, table_ref[0:1])

    @pl.when(pl.program_id(0) == pl.num_programs(0) - 1)
    def _():
        one_ref, two_ref, three_ref = refs[:3]
        small_ref[2:4] = two_ref[0:2]
        small_ref[4:6] = three_ref[0:2]
        small_ref[6:9] = one_ref[2:5]
        small_ref[9:12] = two_ref[2:5]
        small_ref[12:13] = three_ref[2:3]
        small_ref[13:17] = three_ref[8:12]
        if own:
            parts_ref, turned = refs[-2:]
            wide = jnp.concatenate([small_ref[...], jnp.zeros((128 - small_ref.shape[0], small_ref.shape[1]), F32)], 0)
            turned[...] = wide.T
            _, planes, depths = parts_ref.shape[:3]
            for core in range(2):
                for plane in range(planes):
                    for depth in range(depths):
                        base = ((depth ^ place_ref[0]) * planes + (plane ^ place_ref[1])) * 2
                        first = pl.multiple_of((base + (core ^ place_ref[2])) * 16, 16)
                        for half in range(2):
                            rows = turned[pl.ds(pl.multiple_of(first + 8 * half, 8), 8)]
                            parts_ref[core, plane, depth, :, 128 * half : 128 * (half + 1)] = rows


def by_seq(*tail):
    return pl.BlockSpec((1,) + tail, lambda seq, *_: (seq,) + (0,) * len(tail))


def fixed(*shape):
    return pl.BlockSpec(shape, lambda *_: (0,) * len(shape))


def shape_of(shape, dtype):
    return jax.ShapeDtypeStruct(shape, dtype)


def call(kernel, name, work, grid, scalars, args, in_specs, outs, out_specs, scratch):
    return pl.pallas_call(
        kernel,
        out_shape=[shape_of(*out) for out in outs],
        grid_spec=pltpu.PrefetchScalarGridSpec(
            num_scalar_prefetch=len(scalars),
            grid=grid,
            in_specs=in_specs,
            out_specs=out_specs,
            scratch_shapes=scratch,
        ),
        compiler_params=pltpu.CompilerParams(vmem_limit_bytes=LIMIT),
        cost_estimate=pl.CostEstimate(flops=int(work * 1.1e9), bytes_accessed=1 << 20, transcendentals=0),
        name=name,
    )(*scalars, *args)


def self_forward(lengths, grid, x, weights):
    seqs, length, width = x.shape
    shape = x.shape
    block = by_seq(length, width)
    outs = [(shape, LOW)] * 5 + [((seqs, HEADS, length), F32), (shape, F32)]
    out_specs = [block] * 5 + [by_seq(HEADS, length), block]
    scratch = [pltpu.VMEM((length, length), F32), pltpu.VMEM((width, length), F32)]
    if grid.own:
        outs += [((4, width, width), LOW), ((24, width), F32)]
        out_specs += [fixed(4, width, width), fixed(24, width)]
        scratch += [pltpu.VMEM((width, 128), F32)]
    results = call(
        partial(self_forward_kernel, grid.own), "self_forward", 18, (seqs,), (lengths, grid.spot), (x, *weights),
        [block] + [fixed(*part.shape) for part in weights], outs, out_specs, scratch,
    )
    return results if grid.own else (*results, *weights)


def cross_forward(mem_lengths, grid, x, memory, table, weights):
    seqs, length, width = x.shape
    mem_len = memory.shape[1]
    block, mem_block = by_seq(length, width), by_seq(mem_len, width)
    shape, mem_shape = x.shape, memory.shape
    outs = [(shape, LOW), (shape, LOW), (mem_shape, LOW), (mem_shape, LOW), (shape, LOW)]
    outs += [((seqs, HEADS, length), F32), (shape, F32)]
    out_specs = [block, block, mem_block, mem_block, block, by_seq(HEADS, length), block]
    if grid.own:
        outs += [((4, width, width), LOW)]
        out_specs += [fixed(4, width, width)]
    results = call(
        partial(cross_forward_kernel, grid.own), "cross_forward", 24, (seqs,), (mem_lengths, grid.spot),
        (x, memory, table, *weights),
        [block, mem_block, fixed(*table.shape)] + [fixed(*part.shape) for part in weights], outs, out_specs,
        [pltpu.VMEM((mem_len, length), F32), pltpu.VMEM((width, length), F32)],
    )
    return results if grid.own else (*results, *weights)


def ffn(lengths, grid, x, cotangent, table, weights):
    seqs, length, width = x.shape
    blocks = 4
    chunk = grid.hidden // blocks
    bias = table[13:17].reshape(1, grid.hidden)
    act = pltpu.VMEM((seqs, length, width), LOW)
    wide = pltpu.VMEM((seqs, length, chunk), LOW)
    flat = pl.BlockSpec((1, chunk), lambda i, *_: (0, i))
    scratch = [act, act, wide, wide, pltpu.VMEM((seqs, length, width), F32)]
    if grid.own:
        parts = grid.sizes[1::-1] + (8 * grid.own, width)
        grads, grad_specs = [(parts, LOW), (parts, LOW)], [fixed(*parts), fixed(*parts)]
        specs = [fixed(*part.shape) for part in weights]
        scratch += [pltpu.VMEM((width, chunk), F32), pltpu.VMEM((blocks, width, chunk), LOW)]
        scratch += [pltpu.VMEM((grid.hidden, width), LOW)]
    else:
        cols = pl.BlockSpec((width, chunk), lambda i, *_: (0, i))
        rows = pl.BlockSpec((chunk, width), lambda i, *_: (i, 0))
        grads, grad_specs = [(part.shape, F32) for part in weights], [cols, rows]
        specs = [cols, rows]
    return call(
        partial(ffn_kernel, grid.own), "ffn", 24, (blocks,), (lengths, grid.spot),
        (x, cotangent, table, bias, *weights),
        [fixed(*x.shape), fixed(*x.shape), fixed(*table.shape), flat] + specs,
        [(x.shape, F32), (x.shape, F32)] + grads + [((16, width), F32)],
        [fixed(*x.shape), fixed(*x.shape)] + grad_specs + [fixed(16, width)],
        scratch,
    )


def back_call(kernel, name, work, counts, grid, args, in_specs, outs, out_specs, scratch):
    seqs, _, width = args[0].shape
    gw, small = (4, width, width), (8, width)
    outs, out_specs = outs + [(small, F32)], out_specs + [fixed(*small)]
    if grid.own:
        parts = grid.sizes[1::-1] + (4 * grid.own, width)
        outs, out_specs = outs + [(parts, LOW)] * 2, out_specs + [fixed(*parts)] * 2
        scratch = scratch + [pltpu.VMEM(gw, F32)]
    else:
        outs, out_specs = outs + [(gw, F32)], out_specs + [fixed(*gw)]
    return call(
        partial(kernel, grid.own), name, work, (seqs,), (counts, grid.spot), args, in_specs, outs, out_specs, scratch
    )


def cross_back(mem_lengths, grid, grad, x, act, memory, query, key, value, mixed, lse, weights, table):
    seqs, length, width = x.shape
    mem_len = key.shape[1]
    block, mem_block = by_seq(length, width), by_seq(mem_len, width)
    return back_call(
        cross_back_kernel, "cross_back", 30, mem_lengths, grid,
        (grad, x, act, memory, query, key, value, mixed, lse, weights, table),
        [block, block, block, mem_block, block, mem_block, mem_block, block, by_seq(HEADS, length),
         fixed(4, width, width), fixed(*table.shape)],
        [(x.shape, F32), (key.shape, LOW), (key.shape, LOW)],
        [block, mem_block, mem_block],
        [pltpu.VMEM((mem_len, length), F32), pltpu.VMEM((width, length), F32)],
    )


def self_back(lengths, grid, grad, act, query, key, value, mixed, lse, weights):
    seqs, length, width = query.shape
    block = by_seq(length, width)
    return back_call(
        self_back_kernel, "self_back", 22, lengths, grid,
        (grad, act, query, key, value, mixed, lse, weights),
        [block] * 6 + [by_seq(HEADS, length), fixed(4, width, width)],
        [(query.shape, LOW)] * 3, [block] * 3,
        [pltpu.VMEM((length, length), F32), pltpu.VMEM((width, length), F32)],
    )


def memory_grad(gk, gv, weights):
    seqs, mem_len, width = gk.shape
    block = by_seq(mem_len, width)
    return call(
        memory_kernel, "memory_grad", 4, (seqs,), (), (gk, gv, weights),
        [block, block, fixed(4, width, width)], [(gk.shape, F32)], [block], [],
    )[0]


def input_grad(grid, grad, x, gq, gk, gv, weights, table, smalls):
    seqs, length, width = x.shape
    block = by_seq(length, width)
    outs, out_specs, scratch = [(x.shape, F32), ((24, width), F32)], [block, fixed(24, width)], []
    if grid.own:
        parts = (2,) + grid.sizes[1::-1] + (8, 256)
        outs, out_specs, scratch = outs + [(parts, F32)], out_specs + [fixed(*parts)], [pltpu.VMEM((width, 128), F32)]
    return call(
        partial(input_kernel, grid.own), "input_grad", 5, (seqs,), (grid.spot,),
        (grad, x, gq, gk, gv, weights, table, *smalls),
        [block] * 5 + [fixed(4, width, width), fixed(*table.shape)] + [fixed(*small.shape) for small in smalls],
        outs, out_specs, scratch,
    )


def tie(value, *others):
    return lax.optimization_barrier((value, others))[0]


def add_all(parts):
    return sum(part.astype(F32) for part in parts)


class Grid:
    def __init__(self, dp, fsdp, own, hidden):
        self.sizes = (dp, fsdp // 2, 2)
        self.strides = (fsdp, 2, 1)
        self.devices = dp * fsdp
        self.hidden = hidden
        self.own = own if own % 16 == 0 and dp == 4 else 0
        index = lax.axis_index("fsdp")
        self.place = (lax.axis_index("dp"), index >> 1, index & 1)
        self.spot = jnp.stack(self.place).astype(jnp.int32)

    def swap(self, values, stage, step):
        stride = self.strides[stage]
        pairs = [(i, i ^ (step * stride)) for i in range(self.devices)]
        return lax.ppermute(values, AXES, pairs)

    def spread(self, values, stage):
        return jnp.stack(self.send(values, stage))

    def send(self, values, stage):
        return [values] + [self.swap(values, stage, step) for step in range(1, self.sizes[stage])]

    def fetch(self, parts, stage):
        return [parts[0]] + [self.swap(parts[step].astype(LOW), stage, step) for step in range(1, self.sizes[stage])]

    def absolute(self, mine, other):
        depths, planes, _ = self.sizes
        both = jnp.stack([mine, other], 2)
        for axis, stage in ((0, 1), (1, 0), (2, 2)):
            order = jnp.arange(self.sizes[stage]) ^ self.place[stage]
            both = jnp.take(both, order, axis)
        both = jnp.swapaxes(both, 0, 1)
        return both.reshape((self.devices,) + both.shape[3:])

    def relative(self, parts):
        depths, planes, _ = self.sizes
        both = jnp.swapaxes(parts.reshape(self.sizes + parts.shape[1:]), 0, 1)
        for axis, stage in ((0, 1), (1, 0), (2, 2)):
            order = jnp.arange(self.sizes[stage]) ^ self.place[stage]
            both = jnp.take(both, order, axis)
        return both[:, :, 0], both[:, :, 1].astype(LOW)


def adam_update(weight, grad, first, second, clip_scale, step, rate):
    clipped = grad * clip_scale
    first_new = 0.5 * first + 0.5 * clipped
    second_new = 0.55 * second + 0.45 * clipped * clipped
    fix_first = 1.0 - jnp.power(0.5, step)
    fix_second = 1.0 - jnp.power(0.55, step)
    weight_new = weight - rate * (
        first_new / fix_first / (jnp.sqrt(second_new / fix_second) + 1e-08) + 0.01 * weight
    )
    return (weight_new, first_new, second_new)


def local(
    dp,
    fsdp,
    inputs,
    memory,
    cotangent,
    lengths,
    mem_lengths,
    attn_weights,
    ffn_in,
    ffn_out,
    vectors,
    attn_first,
    attn_second,
    ffn_in_first,
    ffn_in_second,
    ffn_out_first,
    ffn_out_second,
    vector_first,
    vector_second,
):
    seqs, length, width = inputs.shape
    own = attn_weights.shape[1]
    hidden = ffn_in.shape[1]
    grid = Grid(dp, fsdp, own, hidden)
    blocks = hidden // width
    out_rows = ffn_out.shape[0]
    count = vectors.shape[0]

    self_low = attn_weights[:4].astype(LOW).reshape(4 * own, width)
    if grid.own:
        turned = jnp.pad(vectors.astype(LOW).T, ((0, 0), (0, 128 - count)))
        turned = jnp.concatenate([turned[:8], turned[8:]], 1)
        extra = jnp.pad(turned, ((0, 0), (0, width - 256)))
    else:
        extra = jnp.pad(vectors.astype(LOW).reshape(1, count * own), ((0, 7), (0, width - count * own)))
    self_chunk = jnp.concatenate([self_low, extra], 0)
    cross_chunk = attn_weights[4:].astype(LOW).reshape(4 * own, width)
    in_blocks = jnp.swapaxes(ffn_in.astype(LOW).reshape(own, blocks, width), 0, 1)
    ffn_chunk = jnp.concatenate([ffn_out.astype(LOW), in_blocks.reshape(blocks * own, width)], 0)

    def attn_whole(mine, other):
        if grid.own:
            return (mine, other)
        full = grid.absolute(mine, other)
        weights = jnp.swapaxes(full[:, : 4 * own].reshape(-1, 4, own, width), 0, 1).reshape(4, width, width)
        table = full[:, 4 * own :].reshape(grid.devices, -1)[:, : count * own]
        if table.size == 0:
            return (weights,)
        table = jnp.swapaxes(table.reshape(-1, count, own), 0, 1).reshape(count, width)
        return (weights, table.astype(F32))

    def ffn_whole(mine, other):
        if grid.own:
            return (mine, other)
        full = grid.absolute(mine, other)
        w_in = full[:, out_rows:].reshape(-1, blocks, own, width)
        return jnp.swapaxes(w_in, 1, 2).reshape(width, hidden), full[:, :out_rows].reshape(hidden, width)

    self_depth = grid.spread(self_chunk, 0)
    late_depth = grid.spread(tie(jnp.concatenate([cross_chunk, ffn_chunk], 0), self_depth), 0)
    self_plane = grid.spread(self_depth, 1)
    self_plane, late_depth = lax.optimization_barrier((self_plane, late_depth))
    cross_parts = grid.send(late_depth[:, : 4 * own], 1)
    first = self_forward(lengths, grid, inputs, attn_whole(self_plane, grid.swap(self_plane, 2, 1)))
    first, cross_parts = lax.optimization_barrier((first, cross_parts))
    act_one, query_one, key_one, value_one, mixed_one, lse_one, resid_one, w_self, table = first
    ffn_parts = grid.send(tie(late_depth[:, 4 * own :], cross_parts), 1)
    cross_plane = jnp.stack(cross_parts)
    second = cross_forward(
        mem_lengths, grid, resid_one, memory, table, attn_whole(cross_plane, grid.swap(cross_plane, 2, 1))
    )
    second, ffn_parts = lax.optimization_barrier((second, ffn_parts))
    act_two, query_two, key_two, value_two, mixed_two, lse_two, resid_two, w_cross = second
    ffn_plane = jnp.stack(ffn_parts)
    output, grad_two, ffn_keep, ffn_send, small_three = ffn(
        lengths, grid, resid_two, cotangent, table, ffn_whole(ffn_plane, grid.swap(ffn_plane, 2, 1))
    )
    if not grid.own:
        parts = jnp.swapaxes(ffn_keep.reshape(grid.devices, own, blocks, width), 1, 2)
        parts = jnp.concatenate(
            [ffn_send.reshape(grid.devices, out_rows, width), parts.reshape(grid.devices, blocks * own, width)], 1
        )
        ffn_keep, ffn_send = grid.relative(parts)

    def attn_parts(grads):
        if grid.own:
            return grads
        parts = jnp.swapaxes(grads[0].reshape(4, grid.devices, own, width), 0, 1)
        return grid.relative(parts.reshape(grid.devices, 4 * own, width))

    def meet(keep, send):
        return keep.astype(F32) + grid.swap(send, 2, 1).astype(F32)

    ffn_sum = meet(ffn_keep, ffn_send)
    grad_two, ffn_sum = lax.optimization_barrier((grad_two, ffn_sum))
    ffn_got = grid.fetch(ffn_sum, 1)
    cross = cross_back(
        mem_lengths, grid, grad_two, resid_one, act_two, memory, query_two, key_two, value_two, mixed_two,
        lse_two, w_cross, table,
    )
    cross, ffn_got = lax.optimization_barrier((cross, ffn_got))
    grad_one, gk_two, gv_two, small_two, *cross_grads = cross
    cross_sum = meet(*attn_parts(cross_grads))
    ffn_sum = add_all(ffn_got)
    grad_one, cross_sum, ffn_sum = lax.optimization_barrier((grad_one, cross_sum, ffn_sum))
    cross_got = grid.fetch(cross_sum, 1)
    state = self_back(
        lengths, grid, grad_one, act_one, query_one, key_one, value_one, mixed_one, lse_one, w_self
    )
    state, cross_got = lax.optimization_barrier((state, cross_got))
    gq_one, gk_one, gv_one, small_one, *self_grads = state
    self_keep, self_send = attn_parts(self_grads)
    late_got = grid.fetch(jnp.concatenate([add_all(cross_got), ffn_sum], 1), 0)
    self_got = grid.swap(self_send, 2, 1)
    grad_one_late = tie(grad_one, self_keep)
    smalls = (small_one, small_two, small_three)
    grad_input, grad_table, *table_parts = input_grad(
        grid, grad_one_late, inputs, gq_one, gk_one, gv_one, w_self, table, smalls
    )
    if grid.own:
        table_keep, table_send = table_parts[0][0], table_parts[0][1]
    else:
        parts = jnp.swapaxes(grad_table[:count].reshape(count, grid.devices, own), 0, 1)
        parts = jnp.pad(parts.reshape(grid.devices, count * own), ((0, 0), (0, -count * own % 256)))
        parts = jnp.pad(parts.reshape(grid.devices, -1, 256), ((0, 0), (0, 7), (0, 0)))[:, :8]
        table_keep, table_send = grid.relative(parts)
    table_sum = table_keep + grid.swap(table_send.astype(LOW), 2, 1).astype(F32)
    self_sum = self_keep.astype(F32) + self_got.astype(F32)
    table_sum = jnp.pad(table_sum, ((0, 0), (0, 0), (0, 0), (0, width - 256)))
    self_sum = jnp.concatenate([self_sum, table_sum], 2)
    last_got = grid.fetch(self_sum, 1)
    last_got, late_got = lax.optimization_barrier((last_got, late_got))
    last_share = add_all(grid.fetch(add_all(last_got), 0))
    late_share = add_all(late_got)
    cross_share, ffn_share = late_share[: 4 * own], late_share[4 * own :]
    self_share = last_share[: 4 * own]
    table_share = last_share[4 * own :, :256]
    if grid.own:
        table_share = jnp.swapaxes(table_share.reshape(8, 2, 128), 0, 1).reshape(own, 128)[:, :count].T
    else:
        table_share = table_share.reshape(-1)[: count * own].reshape(count, own)
    gk_late = tie(gk_two, last_share)
    grad_memory = memory_grad(gk_late, gv_two, w_cross)

    squares = sum(jnp.sum(share * share) for share in (ffn_share, cross_share, self_share, table_share))
    spread = jnp.broadcast_to(squares, (grid.devices, 8, 128))
    total_squares = jnp.sum(lax.all_to_all(spread, AXES, 0, 0)[:, 0, 0])
    grad_norm = jnp.sqrt(total_squares)
    clip_scale = jnp.minimum(1.0, 1.0 / (grad_norm + 1e-06))
    step = jnp.float32(STEP)
    attn_share = jnp.concatenate([self_share, cross_share], 0).reshape(8, own, width)
    in_share = jnp.swapaxes(ffn_share[out_rows:].reshape(blocks, own, width), 0, 1).reshape(own, hidden)
    out_share = ffn_share[:out_rows]
    attn_new = adam_update(attn_weights, attn_share, attn_first, attn_second, clip_scale, step, 0.04)
    first_new = adam_update(ffn_in, in_share, ffn_in_first, ffn_in_second, clip_scale, step, 0.04)
    second_new = adam_update(ffn_out, out_share, ffn_out_first, ffn_out_second, clip_scale, step, 0.04)
    table_new = adam_update(vectors, table_share, vector_first, vector_second, clip_scale, step, 0.25)
    return (
        output,
        grad_input,
        grad_memory,
        grad_norm.reshape(1),
        *attn_new,
        *first_new,
        *second_new,
        *table_new,
    )


def solution(mesh):
    both = ("dp", "fsdp")
    rows = P(both, None, None)
    attn, flat, vec = P(None, both, None), P(both, None), P(None, both)
    return jax.shard_map(
        partial(local, mesh.shape["dp"], mesh.shape["fsdp"]),
        mesh=mesh,
        in_specs=(rows, rows, rows, P(both), P(both), attn, flat, flat, vec)
        + (attn, attn, flat, flat, flat, flat, vec, vec),
        out_specs=(rows, rows, rows, P(), attn, attn, attn) + (flat,) * 6 + (vec,) * 3,
        check_vma=False,
    )
```

```python
from functools import partial

import jax
import jax.numpy as jnp
from jax import lax
from jax.experimental import pallas as pl
from jax.experimental.pallas import tpu as pltpu
from jax.sharding import PartitionSpec as P

HEADS = 8
TILE = 256
FFN_AHEAD = 1
LATE = 1
AHEAD = 2
HEAD_DIM = 64
STEP = 5
AXES = ("dp", "fsdp")
PAIR = 2 * HEAD_DIM
SCALE = HEAD_DIM ** (-0.5)
LOW = jnp.bfloat16
F32 = jnp.float32
LIMIT = 60 * 1024 * 1024


def dot_nn(left, right):
    return lax.dot_general(left, right, (((1,), (0,)), ((), ())), preferred_element_type=F32)


def dot_nt(left, right):
    return lax.dot_general(left, right, (((1,), (1,)), ((), ())), preferred_element_type=F32)


def dot_tn(left, right):
    return lax.dot_general(left, right, (((0,), (0,)), ((), ())), preferred_element_type=F32)


def normalize(values):
    center = values - jnp.mean(values, -1, keepdims=True)
    inverse = lax.rsqrt(jnp.mean(center * center, -1, keepdims=True) + 1e-05)
    return center * inverse, inverse


def normalize_back(grad, hat, inverse, gain):
    grad_hat = grad * (1.0 + gain)
    first = jnp.mean(grad_hat, -1, keepdims=True)
    second = jnp.mean(grad_hat * hat, -1, keepdims=True)
    return inverse * (grad_hat - first - hat * second)


def column_sum(values):
    return jnp.sum(values.astype(F32), 0, keepdims=True)


def own_half(shape, odd):
    lane = lax.broadcasted_iota(jnp.int32, shape, 1)
    return lane >= HEAD_DIM if odd else lane < HEAD_DIM


def half_of(pair, odd, other=0.0):
    return jnp.where(own_half(pair.shape, odd), pair, jnp.asarray(other, pair.dtype))


def spare_column(keys, odd, index, values):
    lane = lax.broadcasted_iota(jnp.int32, (keys, PAIR), 1)
    return jnp.where(lane == index + (0 if odd else HEAD_DIM), values, 0.0)


def key_bias(keys, count):
    key = lax.broadcasted_iota(jnp.int32, (keys, PAIR), 0)
    return jnp.where(key < count, 0.0, -1e30)


def causal_bias(size):
    key = lax.broadcasted_iota(jnp.int32, (size, size), 0)
    query = lax.broadcasted_iota(jnp.int32, (size, size), 1)
    return jnp.where(key <= query, 0.0, -1e30)


def three_parts(row):
    high = row.astype(LOW).astype(F32)
    mid = (row - high).astype(LOW).astype(F32)
    index = lax.broadcasted_iota(jnp.int32, (16, row.shape[1]), 0)
    block = jnp.where(index == 0, high, jnp.where(index == 1, mid, jnp.where(index == 2, row - high - mid, 0.0)))
    return jnp.where(index == 3, 1.0, block).astype(LOW)


def spare_rows(rows, odd, extra):
    zeros = jnp.zeros((HEAD_DIM - 16, rows.shape[1]), rows.dtype)
    return jnp.concatenate([extra, zeros, rows] if odd else [rows, extra, zeros], 0)


def attend(query, key, value, count, causal_ref, mixed_ref, lse_ref):
    value_t = value.T
    keys = key.shape[0]
    bias = key_bias(keys, count)
    patterns = [spare_column(keys, odd, 3, bias).astype(LOW) for odd in range(2)]

    def score(head):
        pair, odd = head // 2, head % 2
        cols = slice(pair * PAIR, (pair + 1) * PAIR)
        left = jnp.where(own_half((keys, PAIR), odd), key[:, cols], patterns[odd])
        scores = dot_nt(left, half_of(query[:, cols] * SCALE, odd, 1.0))
        return scores if causal_ref is None else scores + causal_ref[...]

    def finish(rows, probs):
        mixed_ref[rows] = dot_nn(value_t[rows], probs)

    ahead, late = [score(head) for head in range(AHEAD)], []
    for head in range(HEADS):
        scores = ahead.pop(0)
        if head + AHEAD < HEADS:
            ahead.append(score(head + AHEAD))
        rows = slice(head * HEAD_DIM, (head + 1) * HEAD_DIM)
        top = jnp.max(scores, 0, keepdims=True)
        expo = jnp.exp(scores - top)
        total = jnp.sum(expo, 0, keepdims=True)
        lse_ref[0, head : head + 1] = top + jnp.log(total)
        late.append((rows, (expo * (1.0 / total)).astype(LOW)))
        if len(late) > LATE:
            finish(*late.pop(0))
    for item in late:
        finish(*item)


def attend_back(query_ref, key_ref, value_ref, mixed_ref, grad, count, causal_ref, lse_ref, gq_ref, gk_ref, gv_ref):
    key_t, query_t, grad_t = key_ref[0].T, (query_ref[0] * SCALE).T, grad.T
    keys = key_ref.shape[1]
    bias = key_bias(keys, count)
    lane = lax.broadcasted_iota(jnp.int32, (keys, PAIR), 1)
    patterns = []
    for odd in range(2):
        start = 0 if odd else HEAD_DIM
        ones = jnp.where((lane >= start) & (lane < start + 3), 1.0, 0.0)
        patterns.append((ones + spare_column(keys, odd, 3, bias)).astype(LOW))

    def begin(head):
        pair, odd = head // 2, head % 2
        cols = slice(pair * PAIR, (pair + 1) * PAIR)
        rows = slice(head * HEAD_DIM, (head + 1) * HEAD_DIM)
        scores = dot_nn(
            jnp.where(own_half((keys, PAIR), odd), key_ref[0, :, cols], patterns[odd]),
            spare_rows(query_t[rows], odd, three_parts(-lse_ref[0, head : head + 1])),
        )
        slopes = dot_nn(half_of(value_ref[0, :, cols], odd), grad_t[cols])
        return scores if causal_ref is None else scores + causal_ref[...], slopes

    sums = []

    def finish(head, probs, grad_scores):
        pair, odd = head // 2, head % 2
        cols = slice(pair * PAIR, (pair + 1) * PAIR)
        rows = slice(head * HEAD_DIM, (head + 1) * HEAD_DIM)
        sums.append(
            (dot_nn(probs, half_of(grad[:, cols], odd)),
             dot_nn(grad_scores, half_of(query_ref[0, :, cols] * SCALE, odd)))
        )
        gq_ref[rows] = dot_nn(key_t[rows], grad_scores)
        if odd:
            gv_ref[0, :, cols] = (sums[-2][0] + sums[-1][0]).astype(LOW)
            gk_ref[0, :, cols] = (sums[-2][1] + sums[-1][1]).astype(LOW)

    ahead, late = [begin(head) for head in range(AHEAD)], []
    for head in range(HEADS):
        scores, slopes = ahead.pop(0)
        if head + AHEAD < HEADS:
            ahead.append(begin(head + AHEAD))
        probs = jnp.exp(scores)
        inner = jnp.sum(probs * slopes, 0, keepdims=True)
        grad_scores = (probs * (slopes - inner)).astype(LOW)
        late.append((head, probs.astype(LOW), grad_scores))
        if len(late) > LATE:
            finish(*late.pop(0))
    for item in late:
        finish(*item)


def place_weights(place_ref, mine_ref, other_ref, blocks, outs, turned=None, table_ref=None):
    planes, depths = mine_ref.shape[:2]
    for plane in range(planes):
        for depth in range(depths):
            base = ((depth ^ place_ref[0]) * planes + (plane ^ place_ref[1])) * 2
            for ref, core in ((mine_ref, place_ref[2]), (other_ref, 1 - place_ref[2])):
                for out, row, own, col in blocks:
                    first = pl.multiple_of((base + core) * own, own)
                    piece = ref[plane, depth, row : row + own]
                    if isinstance(col, int):
                        outs[out][col, pl.ds(first, own)] = piece
                    else:
                        outs[out][pl.ds(first, own), col] = piece
                if turned is not None:
                    row = blocks[-1][1] + blocks[-1][2]
                    piece = ref[plane, depth, row : row + 8].astype(F32)
                    first = pl.multiple_of((base + core) * 16, 16)
                    turned[pl.ds(first, 8)] = piece[:, :128]
                    turned[pl.ds(pl.multiple_of(first + 8, 8), 8)] = piece[:, 128:256]
    if turned is not None:
        table_ref[...] = turned[...].T[: table_ref.shape[0]]


def attn_blocks(own):
    return [(0, i * own, own, i) for i in range(4)]


def ffn_blocks(own, out_rows, width, blocks):
    spots = [(1, 0, out_rows, slice(None))]
    return spots + [(0, out_rows + i * own, own, slice(i * width, (i + 1) * width)) for i in range(blocks)]


def self_forward_kernel(own, count_ref, place_ref, x_ref, *refs):
    act_ref, query_ref, key_ref, value_ref, mixed_ref, lse_ref, out_ref = refs[2:9]
    if own:
        w_ref, table_ref, bias, mixed_t, turned = refs[9:]

        @pl.when(pl.program_id(0) == 0)
        def _():
            place_weights(place_ref, refs[0], refs[1], attn_blocks(own), (w_ref,), turned, table_ref)
    else:
        w_ref, table_ref = refs[:2]
        bias, mixed_t = refs[9:]
    count = count_ref[pl.program_id(0)]
    bias[...] = causal_bias(bias.shape[0])
    x = x_ref[0].astype(F32)
    hat, _ = normalize(x)
    act = (hat * (1.0 + table_ref[0:1]) + table_ref[1:2]).astype(LOW)
    act_ref[0] = act
    query = (dot_nn(act, w_ref[0]) + table_ref[6:7]).astype(LOW)
    key = dot_nn(act, w_ref[1]).astype(LOW)
    value = (dot_nn(act, w_ref[2]) + table_ref[7:8]).astype(LOW)
    query_ref[0], key_ref[0], value_ref[0] = query, key, value
    attend(query, key, value, count, bias, mixed_t, lse_ref)
    mixed = mixed_t[...].T.astype(LOW)
    mixed_ref[0] = mixed
    out_ref[0] = x + dot_nn(mixed, w_ref[3]) + table_ref[8:9]


def cross_forward_kernel(own, count_ref, place_ref, x_ref, mem_ref, table_ref, *refs):
    start = 2 if own else 1
    act_ref, query_ref, key_ref, value_ref, mixed_ref, lse_ref, out_ref = refs[start : start + 7]
    if own:
        w_ref, mixed_t = refs[9:]

        @pl.when(pl.program_id(0) == 0)
        def _():
            place_weights(place_ref, refs[0], refs[1], attn_blocks(own), (w_ref,))
    else:
        w_ref = refs[0]
        (mixed_t,) = refs[8:]
    count = count_ref[pl.program_id(0)]
    x = x_ref[0]
    hat, _ = normalize(x)
    act = (hat * (1.0 + table_ref[2:3]) + table_ref[3:4]).astype(LOW)
    act_ref[0] = act
    query = (dot_nn(act, w_ref[0]) + table_ref[9:10]).astype(LOW)
    key = dot_nn(mem_ref[0], w_ref[1]).astype(LOW)
    value = (dot_nn(mem_ref[0], w_ref[2]) + table_ref[10:11]).astype(LOW)
    query_ref[0], key_ref[0], value_ref[0] = query, key, value
    attend(query, key, value, count, None, mixed_t, lse_ref)
    mixed = mixed_t[...].T.astype(LOW)
    mixed_ref[0] = mixed
    out_ref[0] = x + dot_nn(mixed, w_ref[3]) + table_ref[11:12]


def emit(place_ref, rows_ref, keep_ref, send_ref, row, own):
    planes, depths = keep_ref.shape[:2]
    for plane in range(planes):
        for depth in range(depths):
            base = ((depth ^ place_ref[0]) * planes + (plane ^ place_ref[1])) * 2
            for ref, core in ((keep_ref, place_ref[2]), (send_ref, 1 - place_ref[2])):
                first = pl.multiple_of((base + core) * own, own)
                ref[plane, depth, row : row + own] = rows_ref[pl.ds(first, own)].astype(ref.dtype)


def ffn_kernel(own, count_ref, place_ref, x_ref, cot_ref, table_ref, bias_ref, *refs):
    step = pl.program_id(0)
    seqs, length, width = x_ref.shape
    skip = 4 if own else 2
    out_hbm, grad_hbm, small_ref = refs[skip : skip + 3]
    grad_refs = refs[skip + 3 : 2 * skip + 3]
    act, gf, hidden, gpre, back, out, sems = refs[2 * skip + 3 : 2 * skip + 10]
    chunk = hidden.shape[2]

    def valid(seq):
        row = lax.broadcasted_iota(jnp.int32, (length, 1), 0)
        return (row < count_ref[seq]).astype(F32)

    if own:
        w_in_ref, w_out_ref, rows_in, rows_out = refs[2 * skip + 10 :]
        in_mine, in_other, out_mine, out_other = refs[:4]
        out_rows = out_mine.shape[2]
        planes = out_mine.shape[0]
        place_weights(place_ref, in_mine, in_other, [(0, 0, own, slice(None))], (w_in_ref,))
        for plane in range(planes):
            base = (plane ^ place_ref[1]) * 2
            for ref, core in ((out_mine, place_ref[2]), (out_other, 1 - place_ref[2])):
                first = pl.multiple_of((base + core) * out_rows, out_rows)
                w_out_ref[pl.ds(first, out_rows)] = ref[plane, 0]
    else:
        w_in_ref, w_out_ref = refs[:2]

    @pl.when(step == 0)
    def _():
        small_ref[...] = jnp.zeros_like(small_ref)
        for seq in range(seqs):
            x = x_ref[seq]
            hat, _ = normalize(x)
            act[seq] = (hat * (1.0 + table_ref[4:5]) + table_ref[5:6]).astype(LOW)
            grad = (cot_ref[seq].astype(F32) * valid(seq)).astype(LOW)
            gf[seq] = grad
            small_ref[2:3] += column_sum(grad)
            out[seq] = x + table_ref[12:13]
            back[seq] = jnp.zeros_like(back[seq])

    tiles = [(seq, first) for seq in range(seqs) for first in range(0, length, TILE)]

    def begin(tile):
        seq, first = tile
        rows = slice(first, first + TILE)
        pre = dot_nn(act[seq, rows], w_in_ref[...]) + bias_ref[...]
        return tile, pre, dot_nt(gf[seq, rows], w_out_ref[...])

    def finish(tile, unit, grad_pre):
        seq, first = tile
        rows = slice(first, first + TILE)
        out[seq, rows] += dot_nn(unit, w_out_ref[...])
        back[seq, rows] += dot_nt(grad_pre, w_in_ref[...])

    ahead, late = [begin(tile) for tile in tiles[:FFN_AHEAD]], []
    sums = jnp.zeros((1, chunk), F32)
    for index in range(len(tiles)):
        (seq, first), pre, grad_unit = ahead.pop(0)
        if index + FFN_AHEAD < len(tiles):
            ahead.append(begin(tiles[index + FFN_AHEAD]))
        cdf = 0.5 + 0.5 * lax.erf(pre * 0.5**0.5)
        slope = cdf + pre * (jnp.exp(pre * pre * -0.5) * 0.3989422804014327)
        unit = (pre * cdf).astype(LOW)
        grad_pre = (grad_unit * slope).astype(LOW)
        hidden[seq, first : first + TILE] = unit
        gpre[seq, first : first + TILE] = grad_pre
        sums += column_sum(grad_pre)
        late.append(((seq, first), unit, grad_pre))
        if len(late) > LATE:
            finish(*late.pop(0))
    for item in late:
        finish(*item)
    small_ref[pl.ds(8 + step, 1)] = sums
    tokens = seqs * length
    hidden_all, gf_all = hidden[...].reshape(tokens, -1), gf[...].reshape(tokens, -1)
    act_all, gpre_all = act[...].reshape(tokens, -1), gpre[...].reshape(tokens, -1)
    if own:
        in_keep, in_send, out_keep, out_send = grad_refs
        rows_in[...] = dot_tn(act_all, gpre_all)
        rows_out[...] = dot_tn(hidden_all, gf_all)
        emit(place_ref, rows_in, in_keep, in_send, 0, own)
        for plane in range(planes):
            base = (plane ^ place_ref[1]) * 2
            for ref, core in ((out_keep, place_ref[2]), (out_send, 1 - place_ref[2])):
                first = pl.multiple_of((base + core) * out_rows, out_rows)
                ref[plane, 0] = rows_out[pl.ds(first, out_rows)].astype(ref.dtype)
    else:
        grad_refs[0][...] = dot_tn(act_all, gpre_all)
        grad_refs[1][...] = dot_tn(hidden_all, gf_all)

    @pl.when(step == pl.num_programs(0) - 1)
    def _():
        copies = []
        for seq in range(seqs):
            copies.append(pltpu.make_async_copy(out.at[seq], out_hbm.at[seq], sems.at[0, seq]))
            copies[-1].start()
        for seq in range(seqs):
            hat, inverse = normalize(x_ref[seq])
            grad = back[seq]
            small_ref[0:1] += column_sum(grad * hat)
            small_ref[1:2] += column_sum(grad)
            back[seq] = cot_ref[seq].astype(F32) * valid(seq) + normalize_back(
                grad, hat, inverse, table_ref[4:5]
            )
            copies.append(pltpu.make_async_copy(back.at[seq], grad_hbm.at[seq], sems.at[1, seq]))
            copies[-1].start()
        for copy in copies:
            copy.wait()


def begin_sums(*refs):
    @pl.when(pl.program_id(0) == 0)
    def _():
        for ref in refs:
            ref[...] = jnp.zeros_like(ref)


def end_sums(own, place_ref, gw, keep_ref, send_ref):
    @pl.when(pl.program_id(0) == pl.num_programs(0) - 1)
    def _():
        for index in range(4):
            emit(place_ref, gw.at[index], keep_ref, send_ref, index * own, own)


def cross_back_kernel(
    own, count_ref, place_ref, grad_ref, x_ref, act_ref, mem_ref, query_ref, key_ref,
    value_ref, mixed_ref, lse_ref, w_ref, table_ref, *refs,
):
    out_ref, gk_ref, gv_ref, small_ref = refs[:4]
    if own:
        keep_ref, send_ref, gq_t, gw = refs[4:]
    else:
        gw, gq_t = refs[4:]
    begin_sums(gw, small_ref)
    count = count_ref[pl.program_id(0)]
    grad = grad_ref[0]
    low = grad.astype(LOW)
    gw[3] += dot_tn(mixed_ref[0], low)
    small_ref[4:5] += column_sum(low)
    grad_mixed = dot_nt(low, w_ref[3]).astype(LOW)
    attend_back(query_ref, key_ref, value_ref, mixed_ref, grad_mixed, count, None, lse_ref, gq_t, gk_ref, gv_ref)
    gq = (gq_t[...] * SCALE).T.astype(LOW)
    small_ref[2:3] += column_sum(gq)
    small_ref[3:4] += column_sum(gv_ref[0])
    gw[0] += dot_tn(act_ref[0], gq)
    gw[1] += dot_tn(mem_ref[0], gk_ref[0])
    gw[2] += dot_tn(mem_ref[0], gv_ref[0])
    back = dot_nt(gq, w_ref[0])
    hat, inverse = normalize(x_ref[0])
    small_ref[0:1] += column_sum(back * hat)
    small_ref[1:2] += column_sum(back)
    out_ref[0] = grad + normalize_back(back, hat, inverse, table_ref[2:3])
    if own:
        end_sums(own, place_ref, gw, keep_ref, send_ref)


def self_back_kernel(
    own, count_ref, place_ref, grad_ref, act_ref, query_ref, key_ref, value_ref, mixed_ref,
    lse_ref, w_ref, *refs,
):
    gq_ref, gk_ref, gv_ref, small_ref = refs[:4]
    if own:
        keep_ref, send_ref, bias, gq_t, gw = refs[4:]
    else:
        gw, bias, gq_t = refs[4:]
    begin_sums(gw, small_ref)
    count = count_ref[pl.program_id(0)]
    bias[...] = causal_bias(bias.shape[0])
    low = grad_ref[0].astype(LOW)
    gw[3] += dot_tn(mixed_ref[0], low)
    small_ref[4:5] += column_sum(low)
    grad_mixed = dot_nt(low, w_ref[3]).astype(LOW)
    attend_back(query_ref, key_ref, value_ref, mixed_ref, grad_mixed, count, bias, lse_ref, gq_t, gk_ref, gv_ref)
    gq = (gq_t[...] * SCALE).T.astype(LOW)
    gq_ref[0] = gq
    small_ref[2:3] += column_sum(gq)
    small_ref[3:4] += column_sum(gv_ref[0])
    gw[0] += dot_tn(act_ref[0], gq)
    gw[1] += dot_tn(act_ref[0], gk_ref[0])
    gw[2] += dot_tn(act_ref[0], gv_ref[0])
    if own:
        end_sums(own, place_ref, gw, keep_ref, send_ref)


def memory_kernel(gk_ref, gv_ref, w_ref, out_ref):
    out_ref[0] = dot_nt(gk_ref[0], w_ref[1]) + dot_nt(gv_ref[0], w_ref[2])


def input_kernel(own, place_ref, grad_ref, x_ref, gq_ref, gk_ref, gv_ref, w_ref, table_ref, *refs):
    out_ref, small_ref = refs[-4:-2] if own else refs[-2:]
    begin_sums(small_ref)
    back = dot_nt(gq_ref[0], w_ref[0]) + dot_nt(gk_ref[0], w_ref[1]) + dot_nt(gv_ref[0], w_ref[2])
    hat, inverse = normalize(x_ref[0].astype(F32))
    small_ref[0:1] += column_sum(back * hat)
    small_ref[1:2] += column_sum(back)
    out_ref[0] = grad_ref[0] + normalize_back(back, hat, inverse, table_ref[0:1])

    @pl.when(pl.program_id(0) == pl.num_programs(0) - 1)
    def _():
        one_ref, two_ref, three_ref = refs[:3]
        small_ref[2:4] = two_ref[0:2]
        small_ref[4:6] = three_ref[0:2]
        small_ref[6:9] = one_ref[2:5]
        small_ref[9:12] = two_ref[2:5]
        small_ref[12:13] = three_ref[2:3]
        small_ref[13:17] = three_ref[8:12]
        if own:
            parts_ref, turned = refs[-2:]
            wide = jnp.concatenate([small_ref[...], jnp.zeros((128 - small_ref.shape[0], small_ref.shape[1]), F32)], 0)
            turned[...] = wide.T
            _, planes, depths = parts_ref.shape[:3]
            for core in range(2):
                for plane in range(planes):
                    for depth in range(depths):
                        base = ((depth ^ place_ref[0]) * planes + (plane ^ place_ref[1])) * 2
                        first = pl.multiple_of((base + (core ^ place_ref[2])) * 16, 16)
                        for half in range(2):
                            rows = turned[pl.ds(pl.multiple_of(first + 8 * half, 8), 8)]
                            parts_ref[core, plane, depth, :, 128 * half : 128 * (half + 1)] = rows


def by_seq(*tail):
    return pl.BlockSpec((1,) + tail, lambda seq, *_: (seq,) + (0,) * len(tail))


def fixed(*shape):
    return pl.BlockSpec(shape, lambda *_: (0,) * len(shape))


def shape_of(shape, dtype):
    return jax.ShapeDtypeStruct(shape, dtype)


LIMITS = {'self_forward': 20, 'cross_forward': 20, 'ffn': 28, 'cross_back': 26, 'self_back': 20, 'input_grad': 16, 'memory_grad': 16}


def call(kernel, name, work, grid, scalars, args, in_specs, outs, out_specs, scratch):
    return pl.pallas_call(
        kernel,
        out_shape=[shape_of(*out) for out in outs],
        grid_spec=pltpu.PrefetchScalarGridSpec(
            num_scalar_prefetch=len(scalars),
            grid=grid,
            in_specs=in_specs,
            out_specs=out_specs,
            scratch_shapes=scratch,
        ),
        compiler_params=pltpu.CompilerParams(vmem_limit_bytes=LIMITS[name] << 20),
        cost_estimate=pl.CostEstimate(flops=int(work * 1.1e9), bytes_accessed=1 << 20, transcendentals=0),
        name=name,
    )(*scalars, *args)


def self_forward(lengths, grid, x, weights):
    seqs, length, width = x.shape
    shape = x.shape
    block = by_seq(length, width)
    outs = [(shape, LOW)] * 5 + [((seqs, HEADS, length), F32), (shape, F32)]
    out_specs = [block] * 5 + [by_seq(HEADS, length), block]
    scratch = [pltpu.VMEM((length, length), F32), pltpu.VMEM((width, length), F32)]
    if grid.own:
        outs += [((4, width, width), LOW), ((24, width), F32)]
        out_specs += [fixed(4, width, width), fixed(24, width)]
        scratch += [pltpu.VMEM((width, 128), F32)]
    results = call(
        partial(self_forward_kernel, grid.own), "self_forward", 18, (seqs,), (lengths, grid.spot), (x, *weights),
        [block] + [fixed(*part.shape) for part in weights], outs, out_specs, scratch,
    )
    return results if grid.own else (*results, *weights)


def cross_forward(mem_lengths, grid, x, memory, table, weights):
    seqs, length, width = x.shape
    mem_len = memory.shape[1]
    block, mem_block = by_seq(length, width), by_seq(mem_len, width)
    shape, mem_shape = x.shape, memory.shape
    outs = [(shape, LOW), (shape, LOW), (mem_shape, LOW), (mem_shape, LOW), (shape, LOW)]
    outs += [((seqs, HEADS, length), F32), (shape, F32)]
    out_specs = [block, block, mem_block, mem_block, block, by_seq(HEADS, length), block]
    if grid.own:
        outs += [((4, width, width), LOW)]
        out_specs += [fixed(4, width, width)]
    results = call(
        partial(cross_forward_kernel, grid.own), "cross_forward", 24, (seqs,), (mem_lengths, grid.spot),
        (x, memory, table, *weights),
        [block, mem_block, fixed(*table.shape)] + [fixed(*part.shape) for part in weights], outs, out_specs,
        [pltpu.VMEM((width, length), F32)],
    )
    return results if grid.own else (*results, *weights)


def ffn(lengths, grid, x, cotangent, table, weights):
    seqs, length, width = x.shape
    blocks = 4
    chunk = grid.hidden // blocks
    bias = table[13:17].reshape(1, grid.hidden)
    act = pltpu.VMEM((seqs, length, width), LOW)
    wide = pltpu.VMEM((seqs, length, chunk), LOW)
    total = pltpu.VMEM((seqs, length, width), F32)
    flat = pl.BlockSpec((1, chunk), lambda i, *_: (0, i))
    anywhere = pl.BlockSpec(memory_space=pl.ANY)
    scratch = [act, act, wide, wide, total, total, pltpu.SemaphoreType.DMA((2, seqs))]
    if grid.own:
        depths, planes = grid.sizes[:2]
        own, out_rows = grid.own, grid.hidden // grid.devices
        in_parts, out_parts = (planes, depths, blocks * own, width), (planes, depths, out_rows, width)

        def rows_spec(first):
            return pl.BlockSpec((planes, depths, own, width), lambda i, *_: (0, 0, first + i, 0))

        depth_spec = pl.BlockSpec((planes, 1, out_rows, width), lambda i, counts, place: (0, i ^ place[0], 0, 0))
        specs = [rows_spec(out_rows // own)] * 2 + [depth_spec] * 2
        weights = (*weights, *weights)
        grads = [(in_parts, LOW)] * 2 + [(out_parts, LOW)] * 2
        grad_specs = [rows_spec(0)] * 2 + [depth_spec] * 2
        scratch += [pltpu.VMEM((width, chunk), LOW), pltpu.VMEM((chunk, width), LOW)]
        scratch += [pltpu.VMEM((width, chunk), F32), pltpu.VMEM((chunk, width), F32)]
    else:
        cols = pl.BlockSpec((width, chunk), lambda i, *_: (0, i))
        rows = pl.BlockSpec((chunk, width), lambda i, *_: (i, 0))
        grads, grad_specs = [(part.shape, F32) for part in weights], [cols, rows]
        specs = [cols, rows]
    return call(
        partial(ffn_kernel, grid.own), "ffn", 24, (blocks,), (lengths, grid.spot),
        (x, cotangent, table, bias, *weights),
        [fixed(*x.shape), fixed(*x.shape), fixed(*table.shape), flat] + specs,
        [(x.shape, F32), (x.shape, F32), ((16, width), F32)] + grads,
        [anywhere, anywhere, fixed(16, width)] + grad_specs,
        scratch,
    )


def back_call(kernel, name, work, counts, grid, args, in_specs, outs, out_specs, scratch):
    seqs, _, width = args[0].shape
    gw, small = (4, width, width), (8, width)
    outs, out_specs = outs + [(small, F32)], out_specs + [fixed(*small)]
    if grid.own:
        parts = grid.sizes[1::-1] + (4 * grid.own, width)
        outs, out_specs = outs + [(parts, LOW)] * 2, out_specs + [fixed(*parts)] * 2
        scratch = scratch + [pltpu.VMEM(gw, F32)]
    else:
        outs, out_specs = outs + [(gw, F32)], out_specs + [fixed(*gw)]
    return call(
        partial(kernel, grid.own), name, work, (seqs,), (counts, grid.spot), args, in_specs, outs, out_specs, scratch
    )


def cross_back(mem_lengths, grid, grad, x, act, memory, query, key, value, mixed, lse, weights, table):
    seqs, length, width = x.shape
    mem_len = key.shape[1]
    block, mem_block = by_seq(length, width), by_seq(mem_len, width)
    return back_call(
        cross_back_kernel, "cross_back", 30, mem_lengths, grid,
        (grad, x, act, memory, query, key, value, mixed, lse, weights, table),
        [block, block, block, mem_block, block, mem_block, mem_block, block, by_seq(HEADS, length),
         fixed(4, width, width), fixed(*table.shape)],
        [(x.shape, F32), (key.shape, LOW), (key.shape, LOW)],
        [block, mem_block, mem_block],
        [pltpu.VMEM((width, length), F32)],
    )


def self_back(lengths, grid, grad, act, query, key, value, mixed, lse, weights):
    seqs, length, width = query.shape
    block = by_seq(length, width)
    return back_call(
        self_back_kernel, "self_back", 22, lengths, grid,
        (grad, act, query, key, value, mixed, lse, weights),
        [block] * 6 + [by_seq(HEADS, length), fixed(4, width, width)],
        [(query.shape, LOW)] * 3, [block] * 3,
        [pltpu.VMEM((length, length), F32), pltpu.VMEM((width, length), F32)],
    )


def memory_grad(gk, gv, weights):
    seqs, mem_len, width = gk.shape
    block = by_seq(mem_len, width)
    return call(
        memory_kernel, "memory_grad", 4, (seqs,), (), (gk, gv, weights),
        [block, block, fixed(4, width, width)], [(gk.shape, F32)], [block], [],
    )[0]


def input_grad(grid, grad, x, gq, gk, gv, weights, table, smalls):
    seqs, length, width = x.shape
    block = by_seq(length, width)
    outs, out_specs, scratch = [(x.shape, F32), ((24, width), F32)], [block, fixed(24, width)], []
    if grid.own:
        parts = (2,) + grid.sizes[1::-1] + (8, 256)
        outs, out_specs, scratch = outs + [(parts, F32)], out_specs + [fixed(*parts)], [pltpu.VMEM((width, 128), F32)]
    return call(
        partial(input_kernel, grid.own), "input_grad", 5, (seqs,), (grid.spot,),
        (grad, x, gq, gk, gv, weights, table, *smalls),
        [block] * 5 + [fixed(4, width, width), fixed(*table.shape)] + [fixed(*small.shape) for small in smalls],
        outs, out_specs, scratch,
    )


def tie(value, *others):
    return lax.optimization_barrier((value, others))[0]


def add_all(parts):
    return sum(part.astype(F32) for part in parts)


class Grid:
    def __init__(self, dp, fsdp, own, hidden):
        self.sizes = (dp, fsdp // 2, 2)
        self.strides = (fsdp, 2, 1)
        self.devices = dp * fsdp
        self.hidden = hidden
        self.own = own if own % 16 == 0 and dp == 4 else 0
        index = lax.axis_index("fsdp")
        self.place = (lax.axis_index("dp"), index >> 1, index & 1)
        self.spot = jnp.stack(self.place).astype(jnp.int32)

    def swap(self, values, stage, step):
        stride = self.strides[stage]
        pairs = [(i, i ^ (step * stride)) for i in range(self.devices)]
        return lax.ppermute(values, AXES, pairs)

    def spread(self, values, stage):
        return jnp.stack(self.send(values, stage))

    def send(self, values, stage):
        return [values] + [self.swap(values, stage, step) for step in range(1, self.sizes[stage])]

    def fetch(self, parts, stage):
        return [parts[0]] + [self.swap(parts[step].astype(LOW), stage, step) for step in range(1, self.sizes[stage])]

    def absolute(self, mine, other):
        depths, planes, _ = self.sizes
        both = jnp.stack([mine, other], 2)
        for axis, stage in ((0, 1), (1, 0), (2, 2)):
            order = jnp.arange(self.sizes[stage]) ^ self.place[stage]
            both = jnp.take(both, order, axis)
        both = jnp.swapaxes(both, 0, 1)
        return both.reshape((self.devices,) + both.shape[3:])

    def relative(self, parts):
        depths, planes, _ = self.sizes
        both = jnp.swapaxes(parts.reshape(self.sizes + parts.shape[1:]), 0, 1)
        for axis, stage in ((0, 1), (1, 0), (2, 2)):
            order = jnp.arange(self.sizes[stage]) ^ self.place[stage]
            both = jnp.take(both, order, axis)
        return both[:, :, 0], both[:, :, 1].astype(LOW)


def adam_update(weight, grad, first, second, clip_scale, step, rate):
    clipped = grad * clip_scale
    first_new = 0.5 * first + 0.5 * clipped
    second_new = 0.55 * second + 0.45 * clipped * clipped
    fix_first = 1.0 - jnp.power(0.5, step)
    fix_second = 1.0 - jnp.power(0.55, step)
    weight_new = weight - rate * (
        first_new / fix_first / (jnp.sqrt(second_new / fix_second) + 1e-08) + 0.01 * weight
    )
    return (weight_new, first_new, second_new)


def local(
    dp,
    fsdp,
    inputs,
    memory,
    cotangent,
    lengths,
    mem_lengths,
    attn_weights,
    ffn_in,
    ffn_out,
    vectors,
    attn_first,
    attn_second,
    ffn_in_first,
    ffn_in_second,
    ffn_out_first,
    ffn_out_second,
    vector_first,
    vector_second,
):
    seqs, length, width = inputs.shape
    own = attn_weights.shape[1]
    hidden = ffn_in.shape[1]
    grid = Grid(dp, fsdp, own, hidden)
    blocks = hidden // width
    out_rows = ffn_out.shape[0]
    count = vectors.shape[0]

    self_low = attn_weights[:4].astype(LOW).reshape(4 * own, width)
    if grid.own:
        turned = jnp.pad(vectors.astype(LOW).T, ((0, 0), (0, 128 - count)))
        turned = jnp.concatenate([turned[:8], turned[8:]], 1)
        extra = jnp.pad(turned, ((0, 0), (0, width - 256)))
    else:
        extra = jnp.pad(vectors.astype(LOW).reshape(1, count * own), ((0, 7), (0, width - count * own)))
    self_chunk = jnp.concatenate([self_low, extra], 0)
    cross_chunk = attn_weights[4:].astype(LOW).reshape(4 * own, width)
    in_blocks = jnp.swapaxes(ffn_in.astype(LOW).reshape(own, blocks, width), 0, 1)
    ffn_chunk = jnp.concatenate([ffn_out.astype(LOW), in_blocks.reshape(blocks * own, width)], 0)

    def attn_whole(mine, other):
        if grid.own:
            return (mine, other)
        full = grid.absolute(mine, other)
        weights = jnp.swapaxes(full[:, : 4 * own].reshape(-1, 4, own, width), 0, 1).reshape(4, width, width)
        table = full[:, 4 * own :].reshape(grid.devices, -1)[:, : count * own]
        if table.size == 0:
            return (weights,)
        table = jnp.swapaxes(table.reshape(-1, count, own), 0, 1).reshape(count, width)
        return (weights, table.astype(F32))

    def ffn_whole(mine, other):
        if grid.own:
            return (mine, other)
        full = grid.absolute(mine, other)
        w_in = full[:, out_rows:].reshape(-1, blocks, own, width)
        return jnp.swapaxes(w_in, 1, 2).reshape(width, hidden), full[:, :out_rows].reshape(hidden, width)

    self_depth = grid.spread(self_chunk, 0)
    late_depth = grid.spread(tie(jnp.concatenate([cross_chunk, ffn_chunk], 0), self_depth), 0)
    self_plane = grid.spread(self_depth, 1)
    self_plane, late_depth = lax.optimization_barrier((self_plane, late_depth))
    cross_parts = grid.send(late_depth[:, : 4 * own], 1)
    first = self_forward(lengths, grid, inputs, attn_whole(self_plane, grid.swap(self_plane, 2, 1)))
    first, cross_parts = lax.optimization_barrier((first, cross_parts))
    act_one, query_one, key_one, value_one, mixed_one, lse_one, resid_one, w_self, table = first
    ffn_parts = grid.send(tie(late_depth[:, 4 * own :], cross_parts), 1)
    cross_plane = jnp.stack(cross_parts)
    second = cross_forward(
        mem_lengths, grid, resid_one, memory, table, attn_whole(cross_plane, grid.swap(cross_plane, 2, 1))
    )
    second, ffn_parts = lax.optimization_barrier((second, ffn_parts))
    act_two, query_two, key_two, value_two, mixed_two, lse_two, resid_two, w_cross = second
    ffn_plane = jnp.stack(ffn_parts)
    output, grad_two, small_three, *ffn_grads = ffn(
        lengths, grid, resid_two, cotangent, table, ffn_whole(ffn_plane, grid.swap(ffn_plane, 2, 1))
    )
    if not grid.own:
        parts = jnp.swapaxes(ffn_grads[0].reshape(grid.devices, own, blocks, width), 1, 2)
        in_parts = grid.relative(parts.reshape(grid.devices, blocks * own, width))
        ffn_grads = (*in_parts, *grid.relative(ffn_grads[1].reshape(grid.devices, out_rows, width)))

    def attn_parts(grads):
        if grid.own:
            return grads
        parts = jnp.swapaxes(grads[0].reshape(4, grid.devices, own, width), 0, 1)
        return grid.relative(parts.reshape(grid.devices, 4 * own, width))

    def meet(keep, send):
        return keep.astype(F32) + grid.swap(send, 2, 1).astype(F32)

    ffn_sum = jnp.concatenate([meet(*ffn_grads[2:]), meet(*ffn_grads[:2])], 2)
    grad_two, ffn_sum = lax.optimization_barrier((grad_two, ffn_sum))
    ffn_got = grid.fetch(ffn_sum, 1)
    cross = cross_back(
        mem_lengths, grid, grad_two, resid_one, act_two, memory, query_two, key_two, value_two, mixed_two,
        lse_two, w_cross, table,
    )
    cross, ffn_got = lax.optimization_barrier((cross, ffn_got))
    grad_one, gk_two, gv_two, small_two, *cross_grads = cross
    cross_sum = meet(*attn_parts(cross_grads))
    ffn_sum = add_all(ffn_got)
    grad_one, cross_sum, ffn_sum = lax.optimization_barrier((grad_one, cross_sum, ffn_sum))
    cross_got = grid.fetch(cross_sum, 1)
    state = self_back(
        lengths, grid, grad_one, act_one, query_one, key_one, value_one, mixed_one, lse_one, w_self
    )
    state, cross_got = lax.optimization_barrier((state, cross_got))
    gq_one, gk_one, gv_one, small_one, *self_grads = state
    self_keep, self_send = attn_parts(self_grads)
    late_got = grid.fetch(jnp.concatenate([add_all(cross_got), ffn_sum], 1), 0)
    self_got = grid.swap(self_send, 2, 1)
    grad_one_late = tie(grad_one, self_keep)
    smalls = (small_one, small_two, small_three)
    grad_input, grad_table, *table_parts = input_grad(
        grid, grad_one_late, inputs, gq_one, gk_one, gv_one, w_self, table, smalls
    )
    if grid.own:
        table_keep, table_send = table_parts[0][0], table_parts[0][1]
    else:
        parts = jnp.swapaxes(grad_table[:count].reshape(count, grid.devices, own), 0, 1)
        parts = jnp.pad(parts.reshape(grid.devices, count * own), ((0, 0), (0, -count * own % 256)))
        parts = jnp.pad(parts.reshape(grid.devices, -1, 256), ((0, 0), (0, 7), (0, 0)))[:, :8]
        table_keep, table_send = grid.relative(parts)
    table_sum = table_keep + grid.swap(table_send.astype(LOW), 2, 1).astype(F32)
    self_sum = self_keep.astype(F32) + self_got.astype(F32)
    table_sum = jnp.pad(table_sum, ((0, 0), (0, 0), (0, 0), (0, width - 256)))
    self_sum = jnp.concatenate([self_sum, table_sum], 2)
    last_got = grid.fetch(self_sum, 1)
    last_got, late_got = lax.optimization_barrier((last_got, late_got))
    last_share = add_all(grid.fetch(add_all(last_got), 0))
    late_share = add_all(late_got)
    cross_share, ffn_share = late_share[: 4 * own], late_share[4 * own :]
    self_share = last_share[: 4 * own]
    table_share = last_share[4 * own :, :256]
    if grid.own:
        table_share = jnp.swapaxes(table_share.reshape(8, 2, 128), 0, 1).reshape(own, 128)[:, :count].T
    else:
        table_share = table_share.reshape(-1)[: count * own].reshape(count, own)
    gk_late = tie(gk_two, last_share)
    grad_memory = memory_grad(gk_late, gv_two, w_cross)

    squares = sum(jnp.sum(share * share) for share in (ffn_share, cross_share, self_share, table_share))
    spread = jnp.broadcast_to(squares, (grid.devices, 8, 128))
    total_squares = jnp.sum(lax.all_to_all(spread, AXES, 0, 0)[:, 0, 0])
    grad_norm = jnp.sqrt(total_squares)
    clip_scale = jnp.minimum(1.0, 1.0 / (grad_norm + 1e-06))
    step = jnp.float32(STEP)
    attn_share = jnp.concatenate([self_share, cross_share], 0).reshape(8, own, width)
    in_share = jnp.swapaxes(ffn_share[out_rows:].reshape(blocks, own, width), 0, 1).reshape(own, hidden)
    out_share = ffn_share[:out_rows]
    attn_new = adam_update(attn_weights, attn_share, attn_first, attn_second, clip_scale, step, 0.04)
    first_new = adam_update(ffn_in, in_share, ffn_in_first, ffn_in_second, clip_scale, step, 0.04)
    second_new = adam_update(ffn_out, out_share, ffn_out_first, ffn_out_second, clip_scale, step, 0.04)
    table_new = adam_update(vectors, table_share, vector_first, vector_second, clip_scale, step, 0.25)
    return (
        output,
        grad_input,
        grad_memory,
        grad_norm.reshape(1),
        *attn_new,
        *first_new,
        *second_new,
        *table_new,
    )


def solution(mesh):
    both = ("dp", "fsdp")
    rows = P(both, None, None)
    attn, flat, vec = P(None, both, None), P(both, None), P(None, both)
    return jax.shard_map(
        partial(local, mesh.shape["dp"], mesh.shape["fsdp"]),
        mesh=mesh,
        in_specs=(rows, rows, rows, P(both), P(both), attn, flat, flat, vec)
        + (attn, attn, flat, flat, flat, flat, vec, vec),
        out_specs=(rows, rows, rows, P(), attn, attn, attn) + (flat,) * 6 + (vec,) * 3,
        check_vma=False,
    )
```

```python
from functools import partial

import jax
import jax.numpy as jnp
from jax import lax
from jax.experimental import pallas as pl
from jax.experimental.pallas import tpu as pltpu
from jax.sharding import PartitionSpec as P

HEADS = 8
TILE = 256
FFN_AHEAD = 1
LATE = 1
AHEAD = 2
HEAD_DIM = 64
STEP = 5
AXES = ("dp", "fsdp")
PAIR = 2 * HEAD_DIM
SCALE = HEAD_DIM ** (-0.5)
LOW = jnp.bfloat16
F32 = jnp.float32


def dot_nn(left, right):
    return lax.dot_general(left, right, (((1,), (0,)), ((), ())), preferred_element_type=F32)


def dot_nt(left, right):
    return lax.dot_general(left, right, (((1,), (1,)), ((), ())), preferred_element_type=F32)


def dot_tn(left, right):
    return lax.dot_general(left, right, (((0,), (0,)), ((), ())), preferred_element_type=F32)


def normalize(values):
    center = values - jnp.mean(values, -1, keepdims=True)
    inverse = lax.rsqrt(jnp.mean(center * center, -1, keepdims=True) + 1e-05)
    return center * inverse, inverse


def normalize_back(grad, hat, inverse, gain):
    grad_hat = grad * (1.0 + gain)
    first = jnp.mean(grad_hat, -1, keepdims=True)
    second = jnp.mean(grad_hat * hat, -1, keepdims=True)
    return inverse * (grad_hat - first - hat * second)


def column_sum(values):
    return jnp.sum(values.astype(F32), 0, keepdims=True)


def own_half(shape, odd):
    lane = lax.broadcasted_iota(jnp.int32, shape, 1)
    return lane >= HEAD_DIM if odd else lane < HEAD_DIM


def half_of(pair, odd, other=0.0):
    return jnp.where(own_half(pair.shape, odd), pair, jnp.asarray(other, pair.dtype))


def spare_column(keys, odd, index, values):
    lane = lax.broadcasted_iota(jnp.int32, (keys, PAIR), 1)
    return jnp.where(lane == index + (0 if odd else HEAD_DIM), values, 0.0)


def key_bias(keys, count):
    key = lax.broadcasted_iota(jnp.int32, (keys, PAIR), 0)
    return jnp.where(key < count, 0.0, -1e30)


def causal_bias(size):
    key = lax.broadcasted_iota(jnp.int32, (size, size), 0)
    query = lax.broadcasted_iota(jnp.int32, (size, size), 1)
    return jnp.where(key <= query, 0.0, -1e30)


def three_parts(row):
    high = row.astype(LOW).astype(F32)
    mid = (row - high).astype(LOW).astype(F32)
    index = lax.broadcasted_iota(jnp.int32, (16, row.shape[1]), 0)
    block = jnp.where(index == 0, high, jnp.where(index == 1, mid, jnp.where(index == 2, row - high - mid, 0.0)))
    return jnp.where(index == 3, 1.0, block).astype(LOW)


def spare_rows(rows, odd, extra):
    zeros = jnp.zeros((HEAD_DIM - 16, rows.shape[1]), rows.dtype)
    return jnp.concatenate([extra, zeros, rows] if odd else [rows, extra, zeros], 0)


def attend(query, key, value, count, causal_ref, mixed_ref, lse_ref):
    value_t = value.T
    keys = key.shape[0]
    bias = key_bias(keys, count)
    patterns = [spare_column(keys, odd, 3, bias).astype(LOW) for odd in range(2)]

    def score(head):
        pair, odd = head // 2, head % 2
        cols = slice(pair * PAIR, (pair + 1) * PAIR)
        left = jnp.where(own_half((keys, PAIR), odd), key[:, cols], patterns[odd])
        scores = dot_nt(left, half_of(query[:, cols] * SCALE, odd, 1.0))
        return scores if causal_ref is None else scores + causal_ref[...]

    def finish(rows, probs):
        mixed_ref[rows] = dot_nn(value_t[rows], probs)

    ahead, late = [score(head) for head in range(AHEAD)], []
    for head in range(HEADS):
        scores = ahead.pop(0)
        if head + AHEAD < HEADS:
            ahead.append(score(head + AHEAD))
        rows = slice(head * HEAD_DIM, (head + 1) * HEAD_DIM)
        top = jnp.max(scores, 0, keepdims=True)
        expo = jnp.exp(scores - top)
        total = jnp.sum(expo, 0, keepdims=True)
        lse_ref[0, head : head + 1] = top + jnp.log(total)
        late.append((rows, (expo * (1.0 / total)).astype(LOW)))
        if len(late) > LATE:
            finish(*late.pop(0))
    for item in late:
        finish(*item)


def attend_back(query_ref, key_ref, value_ref, mixed_ref, grad, count, causal_ref, lse_ref, gq_ref, gk_ref, gv_ref):
    key_t, query_t, grad_t = key_ref[0].T, (query_ref[0] * SCALE).T, grad.T
    keys = key_ref.shape[1]
    bias = key_bias(keys, count)
    lane = lax.broadcasted_iota(jnp.int32, (keys, PAIR), 1)
    patterns = []
    for odd in range(2):
        start = 0 if odd else HEAD_DIM
        ones = jnp.where((lane >= start) & (lane < start + 3), 1.0, 0.0)
        patterns.append((ones + spare_column(keys, odd, 3, bias)).astype(LOW))

    def begin(head):
        pair, odd = head // 2, head % 2
        cols = slice(pair * PAIR, (pair + 1) * PAIR)
        rows = slice(head * HEAD_DIM, (head + 1) * HEAD_DIM)
        scores = dot_nn(
            jnp.where(own_half((keys, PAIR), odd), key_ref[0, :, cols], patterns[odd]),
            spare_rows(query_t[rows], odd, three_parts(-lse_ref[0, head : head + 1])),
        )
        slopes = dot_nn(half_of(value_ref[0, :, cols], odd), grad_t[cols])
        return scores if causal_ref is None else scores + causal_ref[...], slopes

    sums = []

    def finish(head, probs, grad_scores):
        pair, odd = head // 2, head % 2
        cols = slice(pair * PAIR, (pair + 1) * PAIR)
        rows = slice(head * HEAD_DIM, (head + 1) * HEAD_DIM)
        sums.append(
            (dot_nn(probs, half_of(grad[:, cols], odd)),
             dot_nn(grad_scores, half_of(query_ref[0, :, cols] * SCALE, odd)))
        )
        gq_ref[rows] = dot_nn(key_t[rows], grad_scores)
        if odd:
            gv_ref[0, :, cols] = (sums[-2][0] + sums[-1][0]).astype(LOW)
            gk_ref[0, :, cols] = (sums[-2][1] + sums[-1][1]).astype(LOW)

    ahead, late = [begin(head) for head in range(AHEAD)], []
    for head in range(HEADS):
        scores, slopes = ahead.pop(0)
        if head + AHEAD < HEADS:
            ahead.append(begin(head + AHEAD))
        probs = jnp.exp(scores)
        inner = jnp.sum(probs * slopes, 0, keepdims=True)
        grad_scores = (probs * (slopes - inner)).astype(LOW)
        late.append((head, probs.astype(LOW), grad_scores))
        if len(late) > LATE:
            finish(*late.pop(0))
    for item in late:
        finish(*item)


def place_weights(place_ref, mine_ref, other_ref, blocks, outs, turned=None, table_ref=None):
    planes, depths = mine_ref.shape[:2]
    for plane in range(planes):
        for depth in range(depths):
            base = ((depth ^ place_ref[0]) * planes + (plane ^ place_ref[1])) * 2
            for ref, core in ((mine_ref, place_ref[2]), (other_ref, 1 - place_ref[2])):
                for out, row, own, col in blocks:
                    first = pl.multiple_of((base + core) * own, own)
                    piece = ref[plane, depth, row : row + own]
                    if isinstance(col, int):
                        outs[out][col, pl.ds(first, own)] = piece
                    else:
                        outs[out][pl.ds(first, own), col] = piece
                if turned is not None:
                    row = blocks[-1][1] + blocks[-1][2]
                    piece = ref[plane, depth, row : row + 8].astype(F32)
                    first = pl.multiple_of((base + core) * 16, 16)
                    turned[pl.ds(first, 8)] = piece[:, :128]
                    turned[pl.ds(pl.multiple_of(first + 8, 8), 8)] = piece[:, 128:256]
    if turned is not None:
        table_ref[...] = turned[...].T[: table_ref.shape[0]]


def attn_blocks(own):
    return [(0, i * own, own, i) for i in range(4)]


def ffn_blocks(own, out_rows, width, blocks):
    spots = [(1, 0, out_rows, slice(None))]
    return spots + [(0, out_rows + i * own, own, slice(i * width, (i + 1) * width)) for i in range(blocks)]


def self_forward_kernel(own, count_ref, place_ref, x_ref, *refs):
    act_ref, query_ref, key_ref, value_ref, mixed_ref, lse_ref, out_ref = refs[2:9]
    if own:
        w_ref, table_ref, bias, mixed_t, turned = refs[9:]

        @pl.when(pl.program_id(0) == 0)
        def _():
            place_weights(place_ref, refs[0], refs[1], attn_blocks(own), (w_ref,), turned, table_ref)
    else:
        w_ref, table_ref = refs[:2]
        bias, mixed_t = refs[9:]
    count = count_ref[pl.program_id(0)]
    bias[...] = causal_bias(bias.shape[0])
    x = x_ref[0].astype(F32)
    hat, _ = normalize(x)
    act = (hat * (1.0 + table_ref[0:1]) + table_ref[1:2]).astype(LOW)
    act_ref[0] = act
    query = (dot_nn(act, w_ref[0]) + table_ref[6:7]).astype(LOW)
    key = dot_nn(act, w_ref[1]).astype(LOW)
    value = (dot_nn(act, w_ref[2]) + table_ref[7:8]).astype(LOW)
    query_ref[0], key_ref[0], value_ref[0] = query, key, value
    attend(query, key, value, count, bias, mixed_t, lse_ref)
    mixed = mixed_t[...].T.astype(LOW)
    mixed_ref[0] = mixed
    out_ref[0] = x + dot_nn(mixed, w_ref[3]) + table_ref[8:9]


def cross_forward_kernel(own, count_ref, place_ref, x_ref, mem_ref, table_ref, *refs):
    start = 2 if own else 1
    act_ref, query_ref, key_ref, value_ref, mixed_ref, lse_ref, out_ref = refs[start : start + 7]
    if own:
        w_ref, mixed_t = refs[9:]

        @pl.when(pl.program_id(0) == 0)
        def _():
            place_weights(place_ref, refs[0], refs[1], attn_blocks(own), (w_ref,))
    else:
        w_ref = refs[0]
        (mixed_t,) = refs[8:]
    count = count_ref[pl.program_id(0)]
    x = x_ref[0]
    hat, _ = normalize(x)
    act = (hat * (1.0 + table_ref[2:3]) + table_ref[3:4]).astype(LOW)
    act_ref[0] = act
    query = (dot_nn(act, w_ref[0]) + table_ref[9:10]).astype(LOW)
    key = dot_nn(mem_ref[0], w_ref[1]).astype(LOW)
    value = (dot_nn(mem_ref[0], w_ref[2]) + table_ref[10:11]).astype(LOW)
    query_ref[0], key_ref[0], value_ref[0] = query, key, value
    attend(query, key, value, count, None, mixed_t, lse_ref)
    mixed = mixed_t[...].T.astype(LOW)
    mixed_ref[0] = mixed
    out_ref[0] = x + dot_nn(mixed, w_ref[3]) + table_ref[11:12]


def emit(place_ref, rows_ref, keep_ref, send_ref, row, own):
    planes, depths = keep_ref.shape[:2]
    for plane in range(planes):
        for depth in range(depths):
            base = ((depth ^ place_ref[0]) * planes + (plane ^ place_ref[1])) * 2
            for ref, core in ((keep_ref, place_ref[2]), (send_ref, 1 - place_ref[2])):
                first = pl.multiple_of((base + core) * own, own)
                ref[plane, depth, row : row + own] = rows_ref[pl.ds(first, own)].astype(ref.dtype)


def ffn_kernel(own, count_ref, place_ref, x_ref, cot_ref, table_ref, bias_ref, *refs):
    step = pl.program_id(0)
    seqs, length, width = x_ref.shape
    skip = 4 if own else 2
    out_hbm, grad_hbm, small_ref = refs[skip : skip + 3]
    grad_refs = refs[skip + 3 : 2 * skip + 3]
    act, gf, hidden, gpre, back, out, sems = refs[2 * skip + 3 : 2 * skip + 10]
    chunk = hidden.shape[2]

    def valid(seq):
        row = lax.broadcasted_iota(jnp.int32, (length, 1), 0)
        return (row < count_ref[seq]).astype(F32)

    if own:
        w_in_ref, w_out_ref, rows_in, rows_out = refs[2 * skip + 10 :]
        in_mine, in_other, out_mine, out_other = refs[:4]
        out_rows = out_mine.shape[2]
        planes = out_mine.shape[0]
        place_weights(place_ref, in_mine, in_other, [(0, 0, own, slice(None))], (w_in_ref,))
        for plane in range(planes):
            base = (plane ^ place_ref[1]) * 2
            for ref, core in ((out_mine, place_ref[2]), (out_other, 1 - place_ref[2])):
                first = pl.multiple_of((base + core) * out_rows, out_rows)
                w_out_ref[pl.ds(first, out_rows)] = ref[plane, 0]
    else:
        w_in_ref, w_out_ref = refs[:2]

    @pl.when(step == 0)
    def _():
        small_ref[...] = jnp.zeros_like(small_ref)
        for seq in range(seqs):
            x = x_ref[seq]
            hat, _ = normalize(x)
            act[seq] = (hat * (1.0 + table_ref[4:5]) + table_ref[5:6]).astype(LOW)
            grad = (cot_ref[seq].astype(F32) * valid(seq)).astype(LOW)
            gf[seq] = grad
            small_ref[2:3] += column_sum(grad)
            out[seq] = x + table_ref[12:13]
            back[seq] = jnp.zeros_like(back[seq])

    tiles = [(seq, first) for seq in range(seqs) for first in range(0, length, TILE)]

    def begin(tile):
        seq, first = tile
        rows = slice(first, first + TILE)
        pre = dot_nn(act[seq, rows], w_in_ref[...]) + bias_ref[...]
        return tile, pre, dot_nt(gf[seq, rows], w_out_ref[...])

    def finish(tile, unit, grad_pre):
        seq, first = tile
        rows = slice(first, first + TILE)
        out[seq, rows] += dot_nn(unit, w_out_ref[...])
        back[seq, rows] += dot_nt(grad_pre, w_in_ref[...])

    ahead, late = [begin(tile) for tile in tiles[:FFN_AHEAD]], []
    sums = jnp.zeros((1, chunk), F32)
    for index in range(len(tiles)):
        (seq, first), pre, grad_unit = ahead.pop(0)
        if index + FFN_AHEAD < len(tiles):
            ahead.append(begin(tiles[index + FFN_AHEAD]))
        cdf = 0.5 + 0.5 * lax.erf(pre * 0.5**0.5)
        slope = cdf + pre * (jnp.exp(pre * pre * -0.5) * 0.3989422804014327)
        unit = (pre * cdf).astype(LOW)
        grad_pre = (grad_unit * slope).astype(LOW)
        hidden[seq, first : first + TILE] = unit
        gpre[seq, first : first + TILE] = grad_pre
        sums += column_sum(grad_pre)
        late.append(((seq, first), unit, grad_pre))
        if len(late) > LATE:
            finish(*late.pop(0))
    for item in late:
        finish(*item)
    small_ref[pl.ds(8 + step, 1)] = sums
    tokens = seqs * length
    hidden_all, gf_all = hidden[...].reshape(tokens, -1), gf[...].reshape(tokens, -1)
    act_all, gpre_all = act[...].reshape(tokens, -1), gpre[...].reshape(tokens, -1)
    if own:
        in_keep, in_send, out_keep, out_send = grad_refs
        rows_in[...] = dot_tn(act_all, gpre_all)
        rows_out[...] = dot_tn(hidden_all, gf_all)
        emit(place_ref, rows_in, in_keep, in_send, 0, own)
        for plane in range(planes):
            base = (plane ^ place_ref[1]) * 2
            for ref, core in ((out_keep, place_ref[2]), (out_send, 1 - place_ref[2])):
                first = pl.multiple_of((base + core) * out_rows, out_rows)
                ref[plane, 0] = rows_out[pl.ds(first, out_rows)].astype(ref.dtype)
    else:
        grad_refs[0][...] = dot_tn(act_all, gpre_all)
        grad_refs[1][...] = dot_tn(hidden_all, gf_all)

    @pl.when(step == pl.num_programs(0) - 1)
    def _():
        copies = []
        for seq in range(seqs):
            copies.append(pltpu.make_async_copy(out.at[seq], out_hbm.at[seq], sems.at[0, seq]))
            copies[-1].start()
        for seq in range(seqs):
            hat, inverse = normalize(x_ref[seq])
            grad = back[seq]
            small_ref[0:1] += column_sum(grad * hat)
            small_ref[1:2] += column_sum(grad)
            back[seq] = cot_ref[seq].astype(F32) * valid(seq) + normalize_back(
                grad, hat, inverse, table_ref[4:5]
            )
            copies.append(pltpu.make_async_copy(back.at[seq], grad_hbm.at[seq], sems.at[1, seq]))
            copies[-1].start()
        for copy in copies:
            copy.wait()


def begin_sums(*refs):
    @pl.when(pl.program_id(0) == 0)
    def _():
        for ref in refs:
            ref[...] = jnp.zeros_like(ref)


def end_sums(own, place_ref, gw, keep_ref, send_ref):
    @pl.when(pl.program_id(0) == pl.num_programs(0) - 1)
    def _():
        for index in range(4):
            emit(place_ref, gw.at[index], keep_ref, send_ref, index * own, own)


def cross_back_kernel(
    own, count_ref, place_ref, grad_ref, x_ref, act_ref, mem_ref, query_ref, key_ref,
    value_ref, mixed_ref, lse_ref, w_ref, table_ref, *refs,
):
    out_ref, gk_ref, gv_ref, small_ref = refs[:4]
    if own:
        keep_ref, send_ref, gq_t, gw = refs[4:]
    else:
        gw, gq_t = refs[4:]
    begin_sums(gw, small_ref)
    count = count_ref[pl.program_id(0)]
    grad = grad_ref[0]
    low = grad.astype(LOW)
    gw[3] += dot_tn(mixed_ref[0], low)
    small_ref[4:5] += column_sum(low)
    grad_mixed = dot_nt(low, w_ref[3]).astype(LOW)
    attend_back(query_ref, key_ref, value_ref, mixed_ref, grad_mixed, count, None, lse_ref, gq_t, gk_ref, gv_ref)
    gq = (gq_t[...] * SCALE).T.astype(LOW)
    small_ref[2:3] += column_sum(gq)
    small_ref[3:4] += column_sum(gv_ref[0])
    gw[0] += dot_tn(act_ref[0], gq)
    gw[1] += dot_tn(mem_ref[0], gk_ref[0])
    gw[2] += dot_tn(mem_ref[0], gv_ref[0])
    back = dot_nt(gq, w_ref[0])
    hat, inverse = normalize(x_ref[0])
    small_ref[0:1] += column_sum(back * hat)
    small_ref[1:2] += column_sum(back)
    out_ref[0] = grad + normalize_back(back, hat, inverse, table_ref[2:3])
    if own:
        end_sums(own, place_ref, gw, keep_ref, send_ref)


def self_back_kernel(
    own, count_ref, place_ref, grad_ref, x_ref, act_ref, query_ref, key_ref, value_ref, mixed_ref,
    lse_ref, w_ref, table_ref, two_ref, three_ref, *refs,
):
    out_ref, small_ref = refs[:2]
    if own:
        keep_ref, send_ref, parts_ref, bias, gq_t, gk_ref, gv_ref, gw, turned = refs[2:]
    else:
        gw, bias, gq_t, gk_ref, gv_ref = refs[2:]
    begin_sums(gw, small_ref)
    count = count_ref[pl.program_id(0)]
    bias[...] = causal_bias(bias.shape[0])
    grad = grad_ref[0]
    low = grad.astype(LOW)
    gw[3] += dot_tn(mixed_ref[0], low)
    small_ref[8:9] += column_sum(low)
    grad_mixed = dot_nt(low, w_ref[3]).astype(LOW)
    attend_back(query_ref, key_ref, value_ref, mixed_ref, grad_mixed, count, bias, lse_ref, gq_t, gk_ref, gv_ref)
    gq = (gq_t[...] * SCALE).T.astype(LOW)
    small_ref[6:7] += column_sum(gq)
    small_ref[7:8] += column_sum(gv_ref[0])
    back = dot_nt(gq, w_ref[0]) + dot_nt(gk_ref[0], w_ref[1]) + dot_nt(gv_ref[0], w_ref[2])
    gw[0] += dot_tn(act_ref[0], gq)
    gw[1] += dot_tn(act_ref[0], gk_ref[0])
    gw[2] += dot_tn(act_ref[0], gv_ref[0])
    hat, inverse = normalize(x_ref[0].astype(F32))
    small_ref[0:1] += column_sum(back * hat)
    small_ref[1:2] += column_sum(back)
    out_ref[0] = grad + normalize_back(back, hat, inverse, table_ref[0:1])

    @pl.when(pl.program_id(0) == pl.num_programs(0) - 1)
    def _():
        small_ref[2:4] = two_ref[0:2]
        small_ref[4:6] = three_ref[0:2]
        small_ref[9:12] = two_ref[2:5]
        small_ref[12:13] = three_ref[2:3]
        small_ref[13:17] = three_ref[8:12]
        if own:
            wide = jnp.concatenate([small_ref[...], jnp.zeros((128 - small_ref.shape[0], small_ref.shape[1]), F32)], 0)
            turned[...] = wide.T
            _, planes, depths = parts_ref.shape[:3]
            for core in range(2):
                for plane in range(planes):
                    for depth in range(depths):
                        base = ((depth ^ place_ref[0]) * planes + (plane ^ place_ref[1])) * 2
                        first = pl.multiple_of((base + (core ^ place_ref[2])) * 16, 16)
                        for half in range(2):
                            rows = turned[pl.ds(pl.multiple_of(first + 8 * half, 8), 8)]
                            parts_ref[core, plane, depth, :, 128 * half : 128 * (half + 1)] = rows

    if own:
        end_sums(own, place_ref, gw, keep_ref, send_ref)


def memory_kernel(gk_ref, gv_ref, w_ref, out_ref):
    out_ref[0] = dot_nt(gk_ref[0], w_ref[1]) + dot_nt(gv_ref[0], w_ref[2])


def by_seq(*tail):
    return pl.BlockSpec((1,) + tail, lambda seq, *_: (seq,) + (0,) * len(tail))


def fixed(*shape):
    return pl.BlockSpec(shape, lambda *_: (0,) * len(shape))


def shape_of(shape, dtype):
    return jax.ShapeDtypeStruct(shape, dtype)


LIMITS = {"self_forward": 20, "cross_forward": 20, "ffn": 28, "cross_back": 26, "self_back": 22, "memory_grad": 16}


def call(kernel, name, work, grid, scalars, args, in_specs, outs, out_specs, scratch):
    return pl.pallas_call(
        kernel,
        out_shape=[shape_of(*out) for out in outs],
        grid_spec=pltpu.PrefetchScalarGridSpec(
            num_scalar_prefetch=len(scalars),
            grid=grid,
            in_specs=in_specs,
            out_specs=out_specs,
            scratch_shapes=scratch,
        ),
        compiler_params=pltpu.CompilerParams(vmem_limit_bytes=LIMITS[name] << 20),
        cost_estimate=pl.CostEstimate(flops=int(work * 1.1e9), bytes_accessed=1 << 20, transcendentals=0),
        name=name,
    )(*scalars, *args)


def self_forward(lengths, grid, x, weights):
    seqs, length, width = x.shape
    shape = x.shape
    block = by_seq(length, width)
    outs = [(shape, LOW)] * 5 + [((seqs, HEADS, length), F32), (shape, F32)]
    out_specs = [block] * 5 + [by_seq(HEADS, length), block]
    scratch = [pltpu.VMEM((length, length), F32), pltpu.VMEM((width, length), F32)]
    if grid.own:
        outs += [((4, width, width), LOW), ((24, width), F32)]
        out_specs += [fixed(4, width, width), fixed(24, width)]
        scratch += [pltpu.VMEM((width, 128), F32)]
    results = call(
        partial(self_forward_kernel, grid.own), "self_forward", 18, (seqs,), (lengths, grid.spot), (x, *weights),
        [block] + [fixed(*part.shape) for part in weights], outs, out_specs, scratch,
    )
    return results if grid.own else (*results, *weights)


def cross_forward(mem_lengths, grid, x, memory, table, weights):
    seqs, length, width = x.shape
    mem_len = memory.shape[1]
    block, mem_block = by_seq(length, width), by_seq(mem_len, width)
    shape, mem_shape = x.shape, memory.shape
    outs = [(shape, LOW), (shape, LOW), (mem_shape, LOW), (mem_shape, LOW), (shape, LOW)]
    outs += [((seqs, HEADS, length), F32), (shape, F32)]
    out_specs = [block, block, mem_block, mem_block, block, by_seq(HEADS, length), block]
    if grid.own:
        outs += [((4, width, width), LOW)]
        out_specs += [fixed(4, width, width)]
    results = call(
        partial(cross_forward_kernel, grid.own), "cross_forward", 24, (seqs,), (mem_lengths, grid.spot),
        (x, memory, table, *weights),
        [block, mem_block, fixed(*table.shape)] + [fixed(*part.shape) for part in weights], outs, out_specs,
        [pltpu.VMEM((width, length), F32)],
    )
    return results if grid.own else (*results, *weights)


def ffn(lengths, grid, x, cotangent, table, weights):
    seqs, length, width = x.shape
    blocks = 4
    chunk = grid.hidden // blocks
    bias = table[13:17].reshape(1, grid.hidden)
    act = pltpu.VMEM((seqs, length, width), LOW)
    wide = pltpu.VMEM((seqs, length, chunk), LOW)
    total = pltpu.VMEM((seqs, length, width), F32)
    flat = pl.BlockSpec((1, chunk), lambda i, *_: (0, i))
    anywhere = pl.BlockSpec(memory_space=pl.ANY)
    scratch = [act, act, wide, wide, total, total, pltpu.SemaphoreType.DMA((2, seqs))]
    if grid.own:
        depths, planes = grid.sizes[:2]
        own, out_rows = grid.own, grid.hidden // grid.devices
        in_parts, out_parts = (planes, depths, blocks * own, width), (planes, depths, out_rows, width)

        def rows_spec(first):
            return pl.BlockSpec((planes, depths, own, width), lambda i, *_: (0, 0, first + i, 0))

        depth_spec = pl.BlockSpec((planes, 1, out_rows, width), lambda i, counts, place: (0, i ^ place[0], 0, 0))
        specs = [rows_spec(out_rows // own)] * 2 + [depth_spec] * 2
        weights = (*weights, *weights)
        grads = [(in_parts, LOW)] * 2 + [(out_parts, LOW)] * 2
        grad_specs = [rows_spec(0)] * 2 + [depth_spec] * 2
        scratch += [pltpu.VMEM((width, chunk), LOW), pltpu.VMEM((chunk, width), LOW)]
        scratch += [pltpu.VMEM((width, chunk), F32), pltpu.VMEM((chunk, width), F32)]
    else:
        cols = pl.BlockSpec((width, chunk), lambda i, *_: (0, i))
        rows = pl.BlockSpec((chunk, width), lambda i, *_: (i, 0))
        grads, grad_specs = [(part.shape, F32) for part in weights], [cols, rows]
        specs = [cols, rows]
    return call(
        partial(ffn_kernel, grid.own), "ffn", 24, (blocks,), (lengths, grid.spot),
        (x, cotangent, table, bias, *weights),
        [fixed(*x.shape), fixed(*x.shape), fixed(*table.shape), flat] + specs,
        [(x.shape, F32), (x.shape, F32), ((16, width), F32)] + grads,
        [anywhere, anywhere, fixed(16, width)] + grad_specs,
        scratch,
    )


def back_call(kernel, name, work, counts, grid, args, in_specs, outs, out_specs, scratch):
    seqs, _, width = args[0].shape
    gw, small = (4, width, width), (8, width)
    outs, out_specs = outs + [(small, F32)], out_specs + [fixed(*small)]
    if grid.own:
        parts = grid.sizes[1::-1] + (4 * grid.own, width)
        outs, out_specs = outs + [(parts, LOW)] * 2, out_specs + [fixed(*parts)] * 2
        scratch = scratch + [pltpu.VMEM(gw, F32)]
    else:
        outs, out_specs = outs + [(gw, F32)], out_specs + [fixed(*gw)]
    return call(
        partial(kernel, grid.own), name, work, (seqs,), (counts, grid.spot), args, in_specs, outs, out_specs, scratch
    )


def cross_back(mem_lengths, grid, grad, x, act, memory, query, key, value, mixed, lse, weights, table):
    seqs, length, width = x.shape
    mem_len = key.shape[1]
    block, mem_block = by_seq(length, width), by_seq(mem_len, width)
    return back_call(
        cross_back_kernel, "cross_back", 30, mem_lengths, grid,
        (grad, x, act, memory, query, key, value, mixed, lse, weights, table),
        [block, block, block, mem_block, block, mem_block, mem_block, block, by_seq(HEADS, length),
         fixed(4, width, width), fixed(*table.shape)],
        [(x.shape, F32), (key.shape, LOW), (key.shape, LOW)],
        [block, mem_block, mem_block],
        [pltpu.VMEM((width, length), F32)],
    )


def self_back(lengths, grid, grad, x, act, query, key, value, mixed, lse, weights, table, smalls):
    seqs, length, width = query.shape
    block = by_seq(length, width)
    gw, small = (4, width, width), (24, width)
    outs, out_specs = [(x.shape, F32), (small, F32)], [block, fixed(*small)]
    scratch = [pltpu.VMEM((length, length), F32), pltpu.VMEM((width, length), F32)]
    scratch += [pltpu.VMEM((1, length, width), LOW)] * 2
    if grid.own:
        sides = grid.sizes[1::-1]
        parts, tables = sides + (4 * grid.own, width), (2,) + sides + (8, 256)
        outs += [(parts, LOW)] * 2 + [(tables, F32)]
        out_specs += [fixed(*parts)] * 2 + [fixed(*tables)]
        scratch += [pltpu.VMEM(gw, F32), pltpu.VMEM((width, 128), F32)]
    else:
        outs, out_specs = outs + [(gw, F32)], out_specs + [fixed(*gw)]
    return call(
        partial(self_back_kernel, grid.own), "self_back", 22, (seqs,), (lengths, grid.spot),
        (grad, x, act, query, key, value, mixed, lse, weights, table, *smalls),
        [block] * 7 + [by_seq(HEADS, length), fixed(*gw), fixed(*table.shape)]
        + [fixed(*small_part.shape) for small_part in smalls],
        outs, out_specs, scratch,
    )


def memory_grad(gk, gv, weights):
    seqs, mem_len, width = gk.shape
    block = by_seq(mem_len, width)
    return call(
        memory_kernel, "memory_grad", 4, (seqs,), (), (gk, gv, weights),
        [block, block, fixed(4, width, width)], [(gk.shape, F32)], [block], [],
    )[0]


def half_add(parts, got):
    return [part.astype(F32) + got[index].astype(F32) for index, part in enumerate(parts[0::2])]


def tie(value, *others):
    return lax.optimization_barrier((value, others))[0]


def add_all(parts):
    return sum(part.astype(F32) for part in parts)


class Grid:
    def __init__(self, dp, fsdp, own, hidden):
        self.sizes = (dp, fsdp // 2, 2)
        self.strides = (fsdp, 2, 1)
        self.devices = dp * fsdp
        self.hidden = hidden
        self.own = own if own % 16 == 0 and dp == 4 else 0
        index = lax.axis_index("fsdp")
        self.place = (lax.axis_index("dp"), index >> 1, index & 1)
        self.spot = jnp.stack(self.place).astype(jnp.int32)

    def swap(self, values, stage, step):
        stride = self.strides[stage]
        pairs = [(i, i ^ (step * stride)) for i in range(self.devices)]
        return lax.ppermute(values, AXES, pairs)

    def spread(self, values, stage):
        return jnp.stack(self.send(values, stage))

    def send(self, values, stage):
        return [values] + [self.swap(values, stage, step) for step in range(1, self.sizes[stage])]

    def fetch(self, parts, stage):
        return [parts[0]] + [self.swap(parts[step].astype(LOW), stage, step) for step in range(1, self.sizes[stage])]

    def half_send(self, parts, stage, step):
        return self.swap(jnp.stack([part.astype(LOW) for part in parts[1::2]]), stage, step)

    def absolute(self, mine, other):
        depths, planes, _ = self.sizes
        both = jnp.stack([mine, other], 2)
        for axis, stage in ((0, 1), (1, 0), (2, 2)):
            order = jnp.arange(self.sizes[stage]) ^ self.place[stage]
            both = jnp.take(both, order, axis)
        both = jnp.swapaxes(both, 0, 1)
        return both.reshape((self.devices,) + both.shape[3:])

    def relative(self, parts):
        depths, planes, _ = self.sizes
        both = jnp.swapaxes(parts.reshape(self.sizes + parts.shape[1:]), 0, 1)
        for axis, stage in ((0, 1), (1, 0), (2, 2)):
            order = jnp.arange(self.sizes[stage]) ^ self.place[stage]
            both = jnp.take(both, order, axis)
        return both[:, :, 0], both[:, :, 1].astype(LOW)


def adam_update(weight, grad, first, second, clip_scale, step, rate):
    clipped = grad * clip_scale
    first_new = 0.5 * first + 0.5 * clipped
    second_new = 0.55 * second + 0.45 * clipped * clipped
    fix_first = 1.0 - jnp.power(0.5, step)
    fix_second = 1.0 - jnp.power(0.55, step)
    weight_new = weight - rate * (
        first_new / fix_first / (jnp.sqrt(second_new / fix_second) + 1e-08) + 0.01 * weight
    )
    return (weight_new, first_new, second_new)


def local(
    dp,
    fsdp,
    inputs,
    memory,
    cotangent,
    lengths,
    mem_lengths,
    attn_weights,
    ffn_in,
    ffn_out,
    vectors,
    attn_first,
    attn_second,
    ffn_in_first,
    ffn_in_second,
    ffn_out_first,
    ffn_out_second,
    vector_first,
    vector_second,
):
    seqs, length, width = inputs.shape
    own = attn_weights.shape[1]
    hidden = ffn_in.shape[1]
    grid = Grid(dp, fsdp, own, hidden)
    blocks = hidden // width
    out_rows = ffn_out.shape[0]
    count = vectors.shape[0]

    self_low = attn_weights[:4].astype(LOW).reshape(4 * own, width)
    if grid.own:
        turned = jnp.pad(vectors.astype(LOW).T, ((0, 0), (0, 128 - count)))
        turned = jnp.concatenate([turned[:8], turned[8:]], 1)
        extra = jnp.pad(turned, ((0, 0), (0, width - 256)))
    else:
        extra = jnp.pad(vectors.astype(LOW).reshape(1, count * own), ((0, 7), (0, width - count * own)))
    self_chunk = jnp.concatenate([self_low, extra], 0)
    cross_chunk = attn_weights[4:].astype(LOW).reshape(4 * own, width)
    in_blocks = jnp.swapaxes(ffn_in.astype(LOW).reshape(own, blocks, width), 0, 1)
    ffn_chunk = jnp.concatenate([ffn_out.astype(LOW), in_blocks.reshape(blocks * own, width)], 0)

    def attn_whole(mine, other):
        if grid.own:
            return (mine, other)
        full = grid.absolute(mine, other)
        weights = jnp.swapaxes(full[:, : 4 * own].reshape(-1, 4, own, width), 0, 1).reshape(4, width, width)
        table = full[:, 4 * own :].reshape(grid.devices, -1)[:, : count * own]
        if table.size == 0:
            return (weights,)
        table = jnp.swapaxes(table.reshape(-1, count, own), 0, 1).reshape(count, width)
        return (weights, table.astype(F32))

    def ffn_whole(mine, other):
        if grid.own:
            return (mine, other)
        full = grid.absolute(mine, other)
        w_in = full[:, out_rows:].reshape(-1, blocks, own, width)
        return jnp.swapaxes(w_in, 1, 2).reshape(width, hidden), full[:, :out_rows].reshape(hidden, width)

    self_depth = grid.spread(self_chunk, 0)
    cross_chunk, ffn_chunk, self_depth = lax.optimization_barrier((cross_chunk, ffn_chunk, self_depth))
    self_plane = grid.spread(self_depth, 1)
    cross_parts = grid.send(cross_chunk, 0)
    ffn_got = grid.swap(ffn_chunk, 0, 1)
    cross_parts, self_plane = lax.optimization_barrier((cross_parts, self_plane))
    ffn_got = tie(ffn_got, cross_parts)
    cross_parts = grid.send(jnp.stack(cross_parts), 1)
    ffn_parts = jnp.stack([ffn_chunk, ffn_got])
    ffn_got = grid.swap(ffn_parts, 0, 2)
    first = self_forward(lengths, grid, inputs, attn_whole(self_plane, grid.swap(self_plane, 2, 1)))
    first, cross_parts, ffn_got = lax.optimization_barrier((first, cross_parts, ffn_got))
    ffn_depth = jnp.concatenate([ffn_parts, ffn_got], 0)
    act_one, query_one, key_one, value_one, mixed_one, lse_one, resid_one, w_self, table = first
    ffn_parts = grid.send(tie(ffn_depth, cross_parts), 1)
    cross_plane = jnp.stack(cross_parts)
    second = cross_forward(
        mem_lengths, grid, resid_one, memory, table, attn_whole(cross_plane, grid.swap(cross_plane, 2, 1))
    )
    second, ffn_parts = lax.optimization_barrier((second, ffn_parts))
    act_two, query_two, key_two, value_two, mixed_two, lse_two, resid_two, w_cross = second
    ffn_plane = jnp.stack(ffn_parts)
    output, grad_two, small_three, *ffn_grads = ffn(
        lengths, grid, resid_two, cotangent, table, ffn_whole(ffn_plane, grid.swap(ffn_plane, 2, 1))
    )
    if not grid.own:
        parts = jnp.swapaxes(ffn_grads[0].reshape(grid.devices, own, blocks, width), 1, 2)
        in_parts = grid.relative(parts.reshape(grid.devices, blocks * own, width))
        ffn_grads = (*in_parts, *grid.relative(ffn_grads[1].reshape(grid.devices, out_rows, width)))

    def attn_parts(grads):
        if grid.own:
            return grads
        parts = jnp.swapaxes(grads[0].reshape(4, grid.devices, own, width), 0, 1)
        return grid.relative(parts.reshape(grid.devices, 4 * own, width))

    def meet(keep, send):
        return keep.astype(F32) + grid.swap(send, 2, 1).astype(F32)

    ffn_sum = jnp.concatenate([meet(*ffn_grads[2:]), meet(*ffn_grads[:2])], 2)
    grad_two, ffn_sum = lax.optimization_barrier((grad_two, ffn_sum))
    ffn_got = grid.fetch(ffn_sum, 1)
    cross = cross_back(
        mem_lengths, grid, grad_two, resid_one, act_two, memory, query_two, key_two, value_two, mixed_two,
        lse_two, w_cross, table,
    )
    cross, ffn_got = lax.optimization_barrier((cross, ffn_got))
    grad_one, gk_two, gv_two, small_two, *cross_grads = cross
    cross_sum = meet(*attn_parts(cross_grads))
    ffn_sum = add_all(ffn_got)
    ffn_parts = [ffn_sum[place] for place in range(grid.sizes[0])]
    grad_one, cross_sum, ffn_parts = lax.optimization_barrier((grad_one, cross_sum, ffn_parts))
    ffn_got = grid.half_send(ffn_parts, 0, 1)
    cross_got = grid.fetch(cross_sum, 1)
    state = self_back(
        lengths, grid, grad_one, inputs, act_one, query_one, key_one, value_one, mixed_one, lse_one, w_self,
        table, (small_two, small_three),
    )
    state, cross_got, ffn_got = lax.optimization_barrier((state, cross_got, ffn_got))
    ffn_parts = half_add(ffn_parts, ffn_got)
    grad_input, grad_table, *self_grads = state
    if grid.own:
        self_keep, self_send, table_parts = self_grads
        table_keep, table_send = table_parts[0], table_parts[1]
    else:
        self_keep, self_send = attn_parts(self_grads)
        parts = jnp.swapaxes(grad_table[:count].reshape(count, grid.devices, own), 0, 1)
        parts = jnp.pad(parts.reshape(grid.devices, count * own), ((0, 0), (0, -count * own % 256)))
        parts = jnp.pad(parts.reshape(grid.devices, -1, 256), ((0, 0), (0, 7), (0, 0)))[:, :8]
        table_keep, table_send = grid.relative(parts)
    self_got = grid.swap(self_send, 2, 1)
    late_sum = add_all(cross_got)
    table_sum = table_keep + grid.swap(table_send.astype(LOW), 2, 1).astype(F32)
    self_sum = self_keep.astype(F32) + self_got.astype(F32)
    table_sum = jnp.pad(table_sum, ((0, 0), (0, 0), (0, 0), (0, width - 256)))
    self_sum = jnp.concatenate([self_sum, table_sum], 2)
    self_sum, late_sum, ffn_parts = lax.optimization_barrier((self_sum, late_sum, ffn_parts))
    last_got = grid.fetch(self_sum, 1)
    late_got = grid.fetch(late_sum, 0)
    step = 2
    while step < grid.sizes[0]:
        ffn_got = grid.half_send(ffn_parts, 0, step)
        ffn_parts = half_add(ffn_parts, ffn_got)
        step *= 2
    last_sum = add_all(last_got)
    late_got, ffn_share, last_sum = lax.optimization_barrier((late_got, ffn_parts[0], last_sum))
    last_share = add_all(grid.fetch(last_sum, 0))
    cross_share = add_all(late_got)
    self_share = last_share[: 4 * own]
    table_share = last_share[4 * own :, :256]
    if grid.own:
        table_share = jnp.swapaxes(table_share.reshape(8, 2, 128), 0, 1).reshape(own, 128)[:, :count].T
    else:
        table_share = table_share.reshape(-1)[: count * own].reshape(count, own)
    gk_late = tie(gk_two, last_share)
    grad_memory = memory_grad(gk_late, gv_two, w_cross)

    squares = sum(jnp.sum(share * share) for share in (ffn_share, cross_share, self_share, table_share))
    spread = jnp.broadcast_to(squares, (grid.devices, 8, 128))
    total_squares = jnp.sum(lax.all_to_all(spread, AXES, 0, 0)[:, 0, 0])
    grad_norm = jnp.sqrt(total_squares)
    clip_scale = jnp.minimum(1.0, 1.0 / (grad_norm + 1e-06))
    step = jnp.float32(STEP)
    attn_share = jnp.concatenate([self_share, cross_share], 0).reshape(8, own, width)
    in_share = jnp.swapaxes(ffn_share[out_rows:].reshape(blocks, own, width), 0, 1).reshape(own, hidden)
    out_share = ffn_share[:out_rows]
    attn_new = adam_update(attn_weights, attn_share, attn_first, attn_second, clip_scale, step, 0.04)
    first_new = adam_update(ffn_in, in_share, ffn_in_first, ffn_in_second, clip_scale, step, 0.04)
    second_new = adam_update(ffn_out, out_share, ffn_out_first, ffn_out_second, clip_scale, step, 0.04)
    table_new = adam_update(vectors, table_share, vector_first, vector_second, clip_scale, step, 0.25)
    return (
        output,
        grad_input,
        grad_memory,
        grad_norm.reshape(1),
        *attn_new,
        *first_new,
        *second_new,
        *table_new,
    )


def solution(mesh):
    both = ("dp", "fsdp")
    rows = P(both, None, None)
    attn, flat, vec = P(None, both, None), P(both, None), P(None, both)
    return jax.shard_map(
        partial(local, mesh.shape["dp"], mesh.shape["fsdp"]),
        mesh=mesh,
        in_specs=(rows, rows, rows, P(both), P(both), attn, flat, flat, vec)
        + (attn, attn, flat, flat, flat, flat, vec, vec),
        out_specs=(rows, rows, rows, P(), attn, attn, attn) + (flat,) * 6 + (vec,) * 3,
        check_vma=False,
    )
```
